1024 devices in a mesh: pipe: 8 (over x), expert: 64 (over z, y), tensor: 2 (over core).
Axes of the slice: x: 8, y: 8, z: 8, core: 2. Of those that a mesh axis runs over, the one named last changes fastest.
Arguments:
- in_flight: bfloat16 [8, 4096, 2048], P('pipe', 'expert', 'tensor'), may hold values from -6 to 6
- fresh_batch: bfloat16 [1, 4096, 2048], P(None, 'expert', 'tensor'), may hold values from -6 to 6
- norm_gain: float32 [8, 2048], P('pipe', 'tensor'), may hold values from 0.25 to 1.75
- up_weight: bfloat16 [8, 64, 2048, 768], P('pipe', 'expert', 'tensor'), may hold values from -0.125 to 0.125
- down_weight: bfloat16 [8, 64, 768, 2048], P('pipe', 'expert', None, 'tensor'), may hold values from -0.21875 to 0.21875
- expert_ids: int32 [2, 8, 4096, 8], P(None, 'pipe', 'expert'), may hold values from 0 to 63, all different within a row; in each aligned block of 64 rows (0 to 63, 64 to 127, ..., all dimensions but the last counted through in order) at most 9 rows name the same one
- route_prob: float32 [2, 8, 4096, 8], P(None, 'pipe', 'expert'), may hold values from 0.05 to 1
Outputs:
- section_out: bfloat16 [8, 4096, 2048], P('pipe', 'expert', 'tensor')
The draws below stay inside these ranges and needn't reach their ends.
Inputs may be any that keep to these rules, and one draw needn't show every extreme that they name: `expert_ids`: in each aligned block of 64 tokens (the tokens of one expert index in one tick and section) no expert is named by more than 9 tokens, and some blocks reach it.
All inputs are finite; a program needn't handle non-finite values.
Results may differ from the reference program's by a relative error of at most 0.023.
Values may be sent and summed in bfloat16 or wider, within the bound.
A program may use at most 32 MiB of HBM per device.

```python
import math
import jax
import jax.numpy as jnp
import numpy as np
from jax import lax

D = 2048
HID = 768
TOK = 64
TICKS = 2
EXPERTS = 64
TOPK = 8
CAP = 9
SECTIONS = 8
TOKENS = 4096
N_TENSOR = 2


def spread(key, base_values, column_power, row_power):
    key_one, key_two = jax.random.split(key)
    feature_count = base_values.shape[-1]
    column_ramp = jnp.arange(feature_count, dtype=jnp.float32) / feature_count - 0.5
    columns = 10.0 ** (column_power * column_ramp) * jax.random.uniform(key_one, (feature_count,), jnp.float32, 0.8, 1.25)
    row_scale = 10.0 ** (row_power * jax.random.uniform(key_two, base_values.shape[:-1] + (1,), jnp.float32, -1.0, 1.0))
    return 0.25 * base_values * row_scale * columns


def draw_in_flight(key, part):
    key = jax.random.fold_in(key, 11)
    key_one, key_two = jax.random.split(key)
    full_shape = (SECTIONS, TOKENS, D)
    base_values = jax.random.truncated_normal(key_one, -3.0, 3.0, full_shape, jnp.float32)
    return spread(key_two, base_values, 0.5, 0.3).astype(jnp.bfloat16)


def draw_fresh_batch(key, part):
    key = jax.random.fold_in(key, 12)
    key_one, key_two = jax.random.split(key)
    full_shape = (TICKS - 1, TOKENS, D)
    base_values = jax.random.truncated_normal(key_one, -3.0, 3.0, full_shape, jnp.float32)
    return spread(key_two, base_values, 0.5, 0.3).astype(jnp.bfloat16)


def level_of(stream_key, extent, cuts, low, top_value):
    level, own = 1.0, jax.random.fold_in(stream_key, 6)
    for axis_at, shards_of in cuts:
        steps = jnp.exp(jax.random.uniform(jax.random.fold_in(own, axis_at), (shards_of,), jnp.float32, low / len(cuts), top_value / len(cuts)))
        level = level * jnp.repeat(steps, extent[axis_at] // shards_of).reshape([-1 if axis == axis_at else 1 for axis in range(len(extent))])
    return level


def deal_out(key, own, number, rows, number_of, top, reach, lean):
    order = jax.random.permutation(key, number_of)
    crowded, usual = portions_of(number_of, rows * top, reach, lean, True), portions_of(number_of, rows * top, reach, lean, False)
    places = jnp.arange(number_of)

    def named(lengths, turn):
        used = int((lengths > 0).sum())
        fixed = max(1, used // 4)
        passed = fixed + (places - fixed + turn * (used - fixed)) % max(1, number_of - fixed)
        return jnp.zeros((number_of,), jnp.int32).at[order[jnp.where(places < fixed, places, passed)]].set(jnp.asarray(lengths, jnp.int32))

    lengths = jnp.where(number % 4 == 0, named(crowded, number // 4), named(usual, number - number // 4 - 1))
    mixed = jax.random.permutation(jax.random.fold_in(own, 3), number_of)
    giver, receiver = mixed[0:number_of // 2 * 2:2], mixed[1:number_of // 2 * 2:2]
    slack = jnp.minimum(lengths[giver] - 1, reach - lengths[receiver]) // 2
    slack = jnp.where((giver == order[0]) | (receiver == order[0]) | (lengths[receiver] == 0), 0, jnp.maximum(slack, 0))
    passed = jax.random.randint(jax.random.fold_in(own, 4), (number_of // 2,), 0, 1 << 20) % (slack + 1)
    lengths = lengths.at[giver].add(-passed).at[receiver].add(passed)
    labels = jnp.searchsorted(jnp.cumsum(lengths), jnp.arange(rows * top), side="right").astype(jnp.int32)
    grid = labels.reshape(top, rows).T
    grid = grid[jax.random.permutation(jax.random.fold_in(own, 1), rows)]
    turn = jax.random.randint(jax.random.fold_in(own, 2), (rows, 1), 0, top)
    return jnp.take_along_axis(grid, (jnp.arange(top)[None, :] + turn) % top, axis=1)


def portions_of(count, total, limit, skew, full):
    portions = [(1 << 20) // math.isqrt(rank ** skew) + 1 for rank in range(1, count + 1)]
    largest = limit if full else min(limit, max(-(-total // count), total * portions[0] // sum(portions)))
    least = 1 if total - largest >= count - 1 else 0
    counts, surplus = [largest] + [least] * (count - 1), total - largest - least * (count - 1)
    while surplus > 0:
        candidates = [i for i in range(1, count) if counts[i] < largest] or [i for i in range(1, count) if counts[i] < limit]
        pool, remaining = sum([portions[i] for i in candidates]), surplus
        for i in candidates:
            more = min(limit - counts[i], max(1, remaining * portions[i] // pool), surplus)
            counts[i] = counts[i] + more
            surplus = surplus - more
    return np.array(counts)


def bell_draw(stream_key, extent, width, reach, cuts=(), kind=jnp.bfloat16):
    level = level_of(stream_key, extent, cuts, -0.22, 0.18) if cuts else 1.0
    entries = jax.random.normal(stream_key, extent, jnp.float32) * width * level
    return jnp.minimum(jnp.maximum(entries, -reach), reach).astype(kind)


def setup_inputs(seed: int = 0) -> dict:
    key_of = jax.random.split(jax.random.key(seed), 8)
    in_flight = draw_in_flight(jax.random.fold_in(key_of[7], 71), 0)
    fresh_batch = draw_fresh_batch(jax.random.fold_in(key_of[7], 71), 0)
    norm_gain = jnp.clip(1.0 + 0.15 * jax.random.normal(key_of[2], (SECTIONS, D), jnp.float32), 0.25, 1.75)
    up_weight = bell_draw(key_of[3], (SECTIONS, EXPERTS, D, HID), D ** -0.5, 0.125, ((0, 8), (1, 64), (2, 2)))
    down_weight = bell_draw(key_of[4], (SECTIONS, EXPERTS, HID, D), HID ** -0.5, 0.21875, ((0, 8), (1, 64), (3, 2)))
    expert_ids_keys = jax.random.split(jax.random.fold_in(key_of[5], 1), TICKS * SECTIONS * TOKENS // TOK)
    expert_ids_turns = jax.random.permutation(jax.random.fold_in(key_of[5], 3), TICKS * SECTIONS * TOKENS // TOK)
    expert_ids = jax.vmap(lambda own, number: deal_out(jax.random.fold_in(key_of[5], 2), own, number, TOK, EXPERTS, TOPK, CAP, 2))(expert_ids_keys, expert_ids_turns).reshape((TICKS, SECTIONS, TOKENS, TOPK))
    route_prob = jnp.clip(jnp.exp(math.log(1.0) - 2.9957323 * jax.random.uniform(key_of[6], (TICKS, SECTIONS, TOKENS, TOPK), jnp.float32) ** level_of(key_of[6], (TICKS, SECTIONS, TOKENS, TOPK), ((1, 8), (2, 64)), -0.2, 0.2)), 0.05, 1.0)
    return {"in_flight": in_flight, "fresh_batch": fresh_batch, "norm_gain": norm_gain, "up_weight": up_weight, "down_weight": down_weight, "expert_ids": expert_ids, "route_prob": route_prob}


epsilon = 1e-06

def slot_table(block_ids):
    one_hot = (block_ids[:, :, None] == jnp.arange(EXPERTS, dtype=jnp.int32)[None, None, :]).astype(jnp.int32)
    per_token = lax.optimization_barrier(jnp.sum(one_hot, axis=1))
    earlier = jnp.cumsum(per_token, axis=0) - per_token
    position = jnp.take_along_axis(earlier, block_ids, axis=1)
    return (block_ids * CAP + position).astype(jnp.int32)

def fill_block(scaled_block, slot_index):
    flat_slots = jnp.zeros((EXPERTS * CAP, D), jnp.bfloat16)
    return flat_slots.at[slot_index.reshape(-1)].set(jnp.repeat(scaled_block, TOPK, axis=0))

def pick_rows(source_rows, slot_index):
    return source_rows[slot_index]

def expert_rows(inputs):
    grouped_rows, up_matrix, down_matrix = inputs
    row_count = grouped_rows.shape[0]
    pieces = jnp.einsum('rtd,tdh->trh', grouped_rows.astype(jnp.float32).reshape(row_count, N_TENSOR, D // N_TENSOR), up_matrix.astype(jnp.float32).reshape(N_TENSOR, D // N_TENSOR, HID))
    rounded = lax.optimization_barrier(pieces.astype(jnp.bfloat16))
    upward = lax.optimization_barrier(jnp.sum(rounded.astype(jnp.float32), axis=0))
    hidden = jax.nn.silu(upward).astype(jnp.bfloat16)
    return jnp.dot(hidden, down_matrix, preferred_element_type=jnp.float32).astype(jnp.bfloat16)

def section_step(inputs):
    block_input, gain_row, up_all, down_all, ids_now, prob_now = inputs
    as_float = block_input.astype(jnp.float32)
    mean_square = lax.optimization_barrier(jnp.mean(as_float * as_float, axis=1, keepdims=True))
    scaled = (as_float * lax.rsqrt(mean_square + epsilon) * gain_row[None, :]).astype(jnp.bfloat16)
    blocks = TOKENS // TOK
    block_ids = ids_now.reshape(blocks, TOK, TOPK)
    slot_index = jax.vmap(slot_table)(block_ids)
    filled = jax.vmap(fill_block)(scaled.reshape(blocks, TOK, D), slot_index)
    grouped = filled.reshape(blocks, EXPERTS, CAP, D).transpose(1, 0, 2, 3).reshape(EXPERTS, blocks * CAP, D)
    produced = lax.map(expert_rows, (grouped, up_all, down_all))
    returned = produced.reshape(EXPERTS, blocks, CAP, D).transpose(1, 0, 2, 3).reshape(blocks, EXPERTS * CAP, D)
    picked = jax.vmap(pick_rows)(returned, slot_index)
    weights = prob_now / lax.optimization_barrier(jnp.sum(prob_now, axis=1, keepdims=True))
    mixture = lax.optimization_barrier(jnp.sum(weights.reshape(blocks, TOK, TOPK, 1) * picked.astype(jnp.float32), axis=2)).reshape(TOKENS, D)
    return (as_float + mixture).astype(jnp.bfloat16)

def reference(in_flight, fresh_batch, norm_gain, up_weight, down_weight, expert_ids, route_prob):
    current = in_flight
    for tick_index in range(TICKS):
        if tick_index > 0:
            current = jnp.concatenate([fresh_batch[tick_index - 1][None], current[:-1]], axis=0)
        current = lax.map(section_step, (current, norm_gain, up_weight, down_weight, expert_ids[tick_index], route_prob[tick_index]))
    return current
```

```python
import functools
import jax
import jax.numpy as jnp
from jax import lax
import jax.experimental.pallas as pl
import jax.experimental.pallas.tpu as pltpu
from jax.sharding import PartitionSpec as P

EPS = 1e-06
MESH = pl.DeviceIdType.MESH
F32 = jnp.float32
BF16 = jnp.bfloat16

SIDE = 8
TOK = 64
TOPK = 8
D = 1024
HID = 768
HC = 3
HW = HID // HC
NC = 2
C = D // NC
C2 = C // 2
TICKS = 2

OFFSETS = (0, 1, 7, 2, 6, 3, 5, 4)
POS = {j: p for p, j in enumerate(OFFSETS)}
PARENT = {1: 0, 2: 1, 3: 2, 4: 3, 7: 0, 6: 7, 5: 6}
CHILDREN = {j: tuple(c for c in PARENT if PARENT[c] == j) for j in range(SIDE)}
ARRIVALS = ((1, 7), (2, 6), (3, 5), (4,))


def offset_of(position):
    odd = lax.rem(position, 2) == 1
    return jnp.where(odd, (position + 1) // 2, lax.rem(SIDE - position // 2, SIDE))


def dot(a, b):
    return jnp.dot(a, b, preferred_element_type=F32)


def kernel(
    x_ref, fresh_ref, gain_ref, up_hbm, down_hbm, ids_ref, prob_ref, out_ref,
    wup, wdn, gb, mb, xb, rb, rxb, pacc, ps, pr, hid, ob, oxb, tb, txb, sb, rr,
    sqs, sqr, shs, shr, xn, ms, mr, omat, o8, got, g8t,
    wsem, meta_sem, sq_sem, sh_send, sh_recv, ring_send, ring_recv, main_sem, ext_sem,
    p_sem, rmain_sem, rext_sem, back_send, back_recv,
):
    core = lax.axis_index("tensor")
    expert = lax.axis_index("expert")
    pipe = lax.axis_index("pipe")
    ez, ey = expert // SIDE, lax.rem(expert, SIDE)
    a = (1 - core) * ez + core * ey
    b = (1 - core) * ey + core * ez

    def device_at(da, db):
        ta, tb_ = lax.rem(a + da + SIDE, SIDE), lax.rem(b + db + SIDE, SIDE)
        return {"expert": (1 - core) * (ta * SIDE + tb_) + core * (tb_ * SIDE + ta)}

    def first(da):
        return device_at(da, 0)

    def second(db):
        return device_at(0, db)

    def remote(src, dst, send, recv, device):
        return pltpu.make_async_remote_copy(
            src_ref=src, dst_ref=dst, send_sem=send, recv_sem=recv,
            device_id=device, device_id_type=MESH,
        )

    up_copy = pltpu.make_async_copy(up_hbm, wup, wsem.at[0])
    down_copy = pltpu.make_async_copy(down_hbm, wdn, wsem.at[1])
    up_copy.start()
    down_copy.start()

    barrier = pltpu.get_barrier_semaphore()
    other_core = {"tensor": 1 - core}

    def greet(device):
        pl.semaphore_signal(barrier, inc=1, device_id=device, device_id_type=MESH)

    for d in range(1, SIDE):
        greet(first(d))
        greet(second(d))
    greet(other_core)

    @pl.when(pipe > 0)
    def _():
        greet({"pipe": pipe - 1})

    @pl.when(pipe < lax.axis_size("pipe") - 1)
    def _():
        greet({"pipe": pipe + 1})

    def put_squares(t, x):
        sums = jnp.sum(x * x, axis=1, keepdims=True)
        sqs[t] = jnp.broadcast_to(sums, (TOK, 128))

    def squares_copy(t):
        return remote(sqs.at[t], sqr.at[t], sq_sem.at[t, 0], sq_sem.at[t, 1], other_core)

    def make_meta():
        row = lax.broadcasted_iota(jnp.int32, (SIDE * SIDE, 128), 0)
        ta = lax.rem(a + row // SIDE, SIDE)
        tb_ = lax.rem(b + offset_of(lax.rem(row, SIDE)), SIDE)
        named = (1 - core) * (ta * SIDE + tb_) + core * (tb_ * SIDE + ta)
        r128 = lax.broadcasted_iota(jnp.int32, (128, 128), 0)
        l128 = lax.broadcasted_iota(jnp.int32, (128, 128), 1)
        earlier = jnp.where((r128 < TOK) & (r128 < lax.rem(l128, TOK)), 1.0, 0.0).astype(BF16)
        for t in range(TICKS):
            ids, prob = ids_ref[t], prob_ref[t]
            gate = prob / jnp.sum(prob, axis=0, keepdims=True)
            member = jnp.zeros((SIDE * SIDE, 128), F32)
            gates = jnp.zeros((SIDE * SIDE, 128), F32)
            for k in range(TOPK):
                hit = named == ids[k : k + 1, :]
                member = member + jnp.where(hit, 1.0, 0.0)
                gates = gates + jnp.where(hit, gate[k : k + 1, :], 0.0)
            slots = jnp.where(member > 0.5, dot(member.astype(BF16), earlier), -1.0)
            ms[:, 16 * t : 16 * t + 8, :] = slots.reshape(SIDE, SIDE, 128)
            ms[:, 16 * t + 8 : 16 * t + 16, :] = gates.reshape(SIDE, SIDE, 128)
        mr[0] = ms[0]

    def build_maps(t):
        row = lax.broadcasted_iota(jnp.int32, (128, 128), 0)
        lane = lax.broadcasted_iota(jnp.int32, (128, 128), 1)
        same = (lax.rem(row, 16) // 8) == (lane // TOK)
        slot = lax.rem(row, 8).astype(F32)
        xrow = lax.broadcasted_iota(jnp.int32, (64, 128), 0)
        xlane = lax.broadcasted_iota(jnp.int32, (64, 128), 1)
        low = lax.broadcasted_iota(jnp.int32, (8, 128), 1) < TOK
        for q in range(4):
            slots = jnp.where(low, mr[2 * q, 16 * t : 16 * t + 8, :], mr[2 * q + 1, 16 * t : 16 * t + 8, :])
            gates = jnp.where(low, mr[2 * q, 16 * t + 8 : 16 * t + 16, :], mr[2 * q + 1, 16 * t + 8 : 16 * t + 16, :])
            wide = jnp.concatenate([jnp.broadcast_to(slots[i : i + 1], (16, 128)) for i in range(8)], axis=0)
            wide_gate = jnp.concatenate([jnp.broadcast_to(gates[i : i + 1], (16, 128)) for i in range(8)], axis=0)
            hit = same & (wide == slot)
            omat[t, q] = jnp.where(hit, 1.0, 0.0).astype(BF16)
            got[t, q] = jnp.where(hit, wide_gate, 0.0).T.astype(BF16)
            wide = jnp.concatenate([jnp.broadcast_to(slots[i : i + 1], (8, 128)) for i in range(8)], axis=0)
            wide_gate = jnp.concatenate([jnp.broadcast_to(gates[i : i + 1], (8, 128)) for i in range(8)], axis=0)
            hit = (lax.rem(xrow, 8) == 2 * q + xlane // TOK) & (wide == 8.0)
            o8[t, :, 128 * q : 128 * q + 128] = jnp.where(hit, 1.0, 0.0).astype(BF16)
            spread_gate = jnp.concatenate([jnp.where(hit, wide_gate, 0.0), jnp.zeros((64, 128), F32)], axis=0)
            g8t[t, q] = spread_gate.T.astype(BF16)

    def pack_extra(rows, ref):
        for p in range(SIDE):
            part = rows[8 * p : 8 * p + 8]
            ref[p] = jnp.concatenate([part[:, :C2], part[:, C2:]], axis=0).astype(BF16)

    def unpack_extra(ref):
        parts = []
        for p in range(SIDE):
            part = ref[p].astype(F32)
            parts.append(jnp.concatenate([part[:8], part[8:]], axis=1))
        return jnp.concatenate(parts, axis=0).astype(BF16)

    x0 = x_ref[...].astype(F32)
    put_squares(0, x0)
    make_meta()
    greeted = 2 * (SIDE - 1) + 1 + jnp.where(pipe > 0, 1, 0) + jnp.where(pipe < lax.axis_size("pipe") - 1, 1, 0)
    pl.semaphore_wait(barrier, greeted)
    squares_copy(0).start()
    for j in range(1, SIDE):
        remote(ms.at[j], mr.at[POS[j]], meta_sem.at[0], meta_sem.at[1], first(j)).start()
    xn[...] = x_ref[...]

    for t in range(TICKS):
        if t > 0:
            put_squares(t, xn[...].astype(F32))
            squares_copy(t).start()
        squares_copy(t).wait()
        scale = lax.rsqrt((sqs[t] + sqr[t]) / (2.0 * D) + EPS)[:, :1]

        def ring_copy(k, j):
            parent = PARENT[j]
            return remote(
                gb.at[t, k, pl.ds(POS[parent] * TOK, TOK)], gb.at[t, k, pl.ds(POS[j] * TOK, TOK)],
                ring_send.at[t, k], ring_recv.at[t, k, j], first(j - parent),
            )

        for k in range(NC):
            cols = slice(k * C, k * C + C)
            gb[t, k, :TOK] = (xn[:, cols].astype(F32) * scale * gain_ref[:, cols]).astype(BF16)
            for j in CHILDREN[0]:
                ring_copy(k, j).start()
        if t == 0:
            remote(mr.at[pl.ds(1, 7)], mr.at[pl.ds(1, 7)], meta_sem.at[0], meta_sem.at[1], first(1)).wait_recv()
        build_maps(t)

        for step in range(4):
            for k in range(NC):
                for j in ARRIVALS[step]:
                    ring_copy(k, j).wait_recv()
                    for child in CHILDREN[j]:
                        ring_copy(k, child).start()
            q = step
            for k in range(NC):
                picked = dot(omat[t, q], gb[t, k, 128 * q : 128 * q + 128, :]).astype(BF16).reshape(SIDE, 16, C)
                mb[t, k, q] = picked
                rb[t, k, 0, q] = picked[0]
                for i in range(1, SIDE):
                    p = POS[i]
                    remote(mb.at[t, k, q, p], rb.at[t, k, p, q], main_sem.at[t, k, 0], main_sem.at[t, k, 1], second(i)).start()
                if step == 3:
                    pack_extra(dot(o8[t], gb[t, k]), xb.at[t, k])
                    rxb[t, k, 0] = xb[t, k, 0]
                    for i in range(1, SIDE):
                        p = POS[i]
                        remote(xb.at[t, k, p], rxb.at[t, k, p], ext_sem.at[t, k, 0], ext_sem.at[t, k, 1], second(i)).start()

        if t == 0:
            up_copy.wait()
        for k in range(NC):
            remote(rb.at[t, k, pl.ds(1, 7)], rb.at[t, k, pl.ds(1, 7)], main_sem.at[t, k, 0], main_sem.at[t, k, 1], second(1)).wait_recv()
            remote(rxb.at[t, k, pl.ds(1, 7)], rxb.at[t, k, pl.ds(1, 7)], ext_sem.at[t, k, 0], ext_sem.at[t, k, 1], second(1)).wait_recv()
            rows = rb[t, k].reshape(512, C)
            extra = unpack_extra(rxb.at[t, k])
            for h in range(HC):
                hs = slice(h * HW, h * HW + HW)
                weight = wup[k * C : k * C + C, hs]
                main_part, extra_part = dot(rows, weight), dot(extra, weight)
                if k > 0:
                    main_part = main_part + pacc[:512, hs]
                    extra_part = extra_part + pacc[512:, hs]
                if k < NC - 1:
                    pacc[:512, hs] = main_part
                    pacc[512:, hs] = extra_part
                else:
                    ps[t, h, :512] = main_part.astype(BF16)
                    ps[t, h, 512:] = extra_part.astype(BF16)
                    remote(ps.at[t, h], pr.at[t, h], p_sem.at[t, h, 0], p_sem.at[t, h, 1], other_core).start()
        xrow = lax.broadcasted_iota(jnp.int32, (64, 64), 0)
        xlane = lax.broadcasted_iota(jnp.int32, (64, 64), 1)
        swap = jnp.where(xlane == lax.rem(xrow, 8) * 8 + xrow // 8, 1.0, 0.0).astype(BF16)
        for h in range(HC):
            remote(ps.at[t, h], pr.at[t, h], p_sem.at[t, h, 0], p_sem.at[t, h, 1], other_core).wait_recv()
            theirs = pr[t, h, :512].astype(F32).reshape(SIDE, SIDE, 8, HW)
            for p in range(SIDE):
                total = ps[t, h, 64 * p : 64 * p + 64].astype(F32) + theirs[:, p].reshape(64, HW)
                hid[64 * p : 64 * p + 64, h * HW : h * HW + HW] = (total / (1.0 + jnp.exp(-total))).astype(BF16)
            total = ps[t, h, 512:].astype(F32) + dot(swap, pr[t, h, 512:])
            hid[512:, h * HW : h * HW + HW] = (total / (1.0 + jnp.exp(-total))).astype(BF16)
        if t == 0:
            down_copy.wait()

        for k in range(NC):
            weight = wdn[:, k * C : k * C + C]
            made = dot(hid[:512], weight).astype(BF16).reshape(SIDE, 4, 16, C)
            ob[t, k] = made
            for q in range(4):
                tb[t, k, q, 0] = made[0, q]
            pack_extra(dot(hid[512:], weight), oxb.at[t, k])
            txb[t, k, 0] = oxb[t, k, 0]
            for i in range(1, SIDE):
                p = POS[i]
                remote(ob.at[t, k, p], tb.at[t, k, :, p], rmain_sem.at[t, k, 0], rmain_sem.at[t, k, 1], second(-i)).start()
                remote(oxb.at[t, k, p], txb.at[t, k, p], rext_sem.at[t, k, 0], rext_sem.at[t, k, 1], second(-i)).start()

        def back_copy(k, j):
            return remote(
                sb.at[t, k, j], rr.at[t, k, j], back_send.at[t, k], back_recv.at[t, k, j], first(PARENT[j] - j),
            )

        for q in (3, 2, 1, 0):
            for k in range(NC):
                if q == 3:
                    remote(rb.at[t, k, pl.ds(1, 7)], rb.at[t, k, pl.ds(1, 7)], rmain_sem.at[t, k, 0], rmain_sem.at[t, k, 1], second(1)).wait_recv()
                    remote(txb.at[t, k, pl.ds(1, 7)], txb.at[t, k, pl.ds(1, 7)], rext_sem.at[t, k, 0], rext_sem.at[t, k, 1], second(1)).wait_recv()
                part = dot(got[t, q], tb[t, k, q].reshape(128, C))
                part = part + dot(g8t[t, q][:, :64], unpack_extra(txb.at[t, k]))
                for h in (1, 0):
                    j = OFFSETS[2 * q + h]
                    total = part[64 * h : 64 * h + 64]
                    for child in CHILDREN[j]:
                        back_copy(k, child).wait_recv()
                        total = total + rr[t, k, child].astype(F32)
                    if j > 0:
                        sb[t, k, j] = total.astype(BF16)
                        back_copy(k, j).start()
                    else:
                        cols = slice(k * C, k * C + C)
                        y = (xn[:, cols].astype(F32) + total).astype(BF16)
                        if t == TICKS - 1:
                            out_ref[:, cols] = y
                        else:
                            shs[t, k] = y

                            @pl.when(pipe < lax.axis_size("pipe") - 1)
                            def _():
                                remote(shs.at[t, k], shr.at[t, k], sh_send.at[t, k], sh_recv.at[t, k], {"pipe": pipe + 1}).start()

        if t < TICKS - 1:
            @pl.when(pipe > 0)
            def _():
                for k in range(NC):
                    remote(shs.at[t, k], shr.at[t, k], sh_send.at[t, k], sh_recv.at[t, k], {"pipe": pipe - 1}).wait_recv()
                    xn[:, k * C : k * C + C] = shr[t, k]

            @pl.when(pipe == 0)
            def _():
                xn[...] = fresh_ref[t]

    remote(mr.at[pl.ds(1, 7)], mr.at[pl.ds(1, 7)], meta_sem.at[0], meta_sem.at[1], first(1)).wait_send()
    for t in range(TICKS):
        for k in range(NC):
            seven = pl.ds(1, 7)
            remote(gb.at[t, k, pl.ds(64, 448)], gb.at[t, k, pl.ds(64, 448)], ring_send.at[t, k], ring_recv.at[t, k, 0], first(1)).wait_send()
            remote(rb.at[t, k, seven], rb.at[t, k, seven], main_sem.at[t, k, 0], main_sem.at[t, k, 1], second(1)).wait_send()
            remote(rxb.at[t, k, seven], rxb.at[t, k, seven], ext_sem.at[t, k, 0], ext_sem.at[t, k, 1], second(1)).wait_send()
            remote(rb.at[t, k, seven], rb.at[t, k, seven], rmain_sem.at[t, k, 0], rmain_sem.at[t, k, 1], second(1)).wait_send()
            remote(txb.at[t, k, seven], txb.at[t, k, seven], rext_sem.at[t, k, 0], rext_sem.at[t, k, 1], second(1)).wait_send()
            remote(sb.at[t, k, seven], sb.at[t, k, seven], back_send.at[t, k], back_recv.at[t, k, 0], first(1)).wait_send()
        for h in range(HC):
            remote(ps.at[t, h], pr.at[t, h], p_sem.at[t, h, 0], p_sem.at[t, h, 1], other_core).wait_send()

    @pl.when(pipe < lax.axis_size("pipe") - 1)
    def _():
        for t in range(TICKS - 1):
            for k in range(NC):
                remote(shs.at[t, k], shr.at[t, k], sh_send.at[t, k], sh_recv.at[t, k], {"pipe": pipe + 1}).wait_send()


def on_device(in_flight, fresh_batch, norm_gain, up_weight, down_weight, expert_ids, route_prob):
    ids = jnp.swapaxes(expert_ids[:, 0], 1, 2)
    ids = jnp.concatenate([ids, ids], axis=2)
    prob = jnp.swapaxes(route_prob[:, 0], 1, 2)
    prob = jnp.concatenate([prob, prob], axis=2)
    vmem = pl.BlockSpec(memory_space=pltpu.VMEM)
    hbm = pl.BlockSpec(memory_space=pl.ANY)
    dma = pltpu.SemaphoreType.DMA
    scratch = [
        pltpu.VMEM((D, HID), BF16), pltpu.VMEM((HID, D), BF16),
        pltpu.VMEM((TICKS, NC, 512, C), BF16),
        pltpu.VMEM((TICKS, NC, 4, SIDE, 16, C), BF16),
        pltpu.VMEM((TICKS, NC, SIDE, 16, C2), BF16),
        pltpu.VMEM((TICKS, NC, SIDE, 4, 16, C), BF16),
        pltpu.VMEM((TICKS, NC, SIDE, 16, C2), BF16),
        pltpu.VMEM((576, HID), F32),
        pltpu.VMEM((TICKS, HC, 576, HW), BF16),
        pltpu.VMEM((TICKS, HC, 576, HW), BF16),
        pltpu.VMEM((576, HID), BF16),
        pltpu.VMEM((TICKS, NC, SIDE, 4, 16, C), BF16),
        pltpu.VMEM((TICKS, NC, SIDE, 16, C2), BF16),
        pltpu.VMEM((TICKS, NC, 4, SIDE, 16, C), BF16),
        pltpu.VMEM((TICKS, NC, SIDE, 16, C2), BF16),
        pltpu.VMEM((TICKS, NC, SIDE, TOK, C), BF16),
        pltpu.VMEM((TICKS, NC, SIDE, TOK, C), BF16),
        pltpu.VMEM((TICKS, TOK, 128), F32),
        pltpu.VMEM((TICKS, TOK, 128), F32),
        pltpu.VMEM((TICKS, NC, TOK, C), BF16),
        pltpu.VMEM((TICKS, NC, TOK, C), BF16),
        pltpu.VMEM((TOK, D), BF16),
        pltpu.VMEM((SIDE, 32, 128), F32),
        pltpu.VMEM((SIDE, 32, 128), F32),
        pltpu.VMEM((TICKS, 4, 128, 128), BF16),
        pltpu.VMEM((TICKS, 64, 512), BF16),
        pltpu.VMEM((TICKS, 4, 128, 128), BF16),
        pltpu.VMEM((TICKS, 4, 128, 128), BF16),
        dma((2,)), dma((2,)), dma((TICKS, 2)), dma((TICKS, NC)), dma((TICKS, NC)),
        dma((TICKS, NC)), dma((TICKS, NC, SIDE)), dma((TICKS, NC, 2)), dma((TICKS, NC, 2)),
        dma((TICKS, HC, 2)), dma((TICKS, NC, 2)), dma((TICKS, NC, 2)),
        dma((TICKS, NC)), dma((TICKS, NC, SIDE)),
    ]
    y = pl.pallas_call(
        kernel,
        name="window",
        out_shape=jax.ShapeDtypeStruct((TOK, D), BF16),
        in_specs=[vmem, vmem, vmem, hbm, hbm, vmem, vmem],
        out_specs=vmem,
        scratch_shapes=scratch,
        compiler_params=pltpu.CompilerParams(
            collective_id=0, has_side_effects=True, vmem_limit_bytes=48 * 2**20
        ),
    )(in_flight[0], fresh_batch, norm_gain, up_weight[0, 0], down_weight[0, 0], ids, prob)
    return y[None]


def solution(mesh):
    placed = (
        P("pipe", "expert", "tensor"),
        P(None, "expert", "tensor"),
        P("pipe", "tensor"),
        P("pipe", "expert", "tensor", None),
        P("pipe", "expert", None, "tensor"),
        P(None, "pipe", "expert", None),
        P(None, "pipe", "expert", None),
    )
    return jax.shard_map(
        on_device,
        mesh=mesh,
        in_specs=placed,
        out_specs=P("pipe", "expert", "tensor"),
        check_vma=False,
    )
```

```python
import functools
import jax
import jax.numpy as jnp
from jax import lax
import jax.experimental.pallas as pl
import jax.experimental.pallas.tpu as pltpu
from jax.sharding import PartitionSpec as P

EPS = 1e-06
MESH = pl.DeviceIdType.MESH
F32 = jnp.float32
BF16 = jnp.bfloat16

SIDE = 8
TOK = 64
TOPK = 8
D = 1024
HID = 768
NC = 2
C = D // NC
C2 = C // 2
TICKS = 2

OFFSETS = (0, 1, 7, 2, 6, 3, 5, 4)
POS = {j: p for p, j in enumerate(OFFSETS)}
PARENT = {1: 0, 2: 1, 3: 2, 4: 3, 7: 0, 6: 7, 5: 6}
CHILDREN = {j: tuple(c for c in PARENT if PARENT[c] == j) for j in range(SIDE)}
ARRIVALS = ((1, 7), (2, 6), (3, 5), (4,))
FAR_FIRST = (4, 3, 5, 2, 6, 1, 7)


def offset_of(position):
    odd = lax.rem(position, 2) == 1
    return jnp.where(odd, (position + 1) // 2, lax.rem(SIDE - position // 2, SIDE))


def dot(a, b):
    return jnp.dot(a, b, preferred_element_type=F32)


def kernel(
    x_hbm, fresh_hbm, gain_hbm, up_hbm, down_hbm, ids_hbm, prob_hbm, out_ref,
    xn, fresh_ref, gain_ref, wup, wdn, ids_ref, prob_ref,
    gb, mb, xb, rb, rxb, ps, pr, pse, pre, ob, oxb, tb, txb, te, sb, rr,
    sqs, sqr, shs, shr, ms, mr, omat, o8, got, g8t,
    load_sem, meta_sem, sq_sem, sh_send, sh_recv, ring_send, ring_recv, main_send, main_recv, ext_sem,
    p_sem, pe_sem, rmain_send, rmain_recv, rext_sem, back_send, back_recv,
):
    core = lax.axis_index("tensor")
    expert = lax.axis_index("expert")
    pipe = lax.axis_index("pipe")
    ez, ey = expert // SIDE, lax.rem(expert, SIDE)
    a = (1 - core) * ez + core * ey
    b = (1 - core) * ey + core * ez

    def device_at(da, db):
        ta, tb_ = lax.rem(a + da + SIDE, SIDE), lax.rem(b + db + SIDE, SIDE)
        return {"expert": (1 - core) * (ta * SIDE + tb_) + core * (tb_ * SIDE + ta)}

    def first(da):
        return device_at(da, 0)

    def second(db):
        return device_at(0, db)

    def remote(src, dst, send, recv, device):
        return pltpu.make_async_remote_copy(
            src_ref=src, dst_ref=dst, send_sem=send, recv_sem=recv,
            device_id=device, device_id_type=MESH,
        )

    loads = [
        pltpu.make_async_copy(source, held, load_sem.at[n])
        for n, (source, held) in enumerate((
            (x_hbm, xn), (ids_hbm, ids_ref), (prob_hbm, prob_ref), (gain_hbm, gain_ref),
            (fresh_hbm, fresh_ref), (up_hbm, wup), (down_hbm, wdn),
        ))
    ]
    for load in loads:
        load.start()
    x_load, ids_load, prob_load, gain_load, fresh_load, up_load, down_load = loads

    barrier = pltpu.get_barrier_semaphore()
    other_core = {"tensor": 1 - core}

    def greet(device):
        pl.semaphore_signal(barrier, inc=1, device_id=device, device_id_type=MESH)

    for d in range(1, SIDE):
        greet(first(d))
        greet(second(d))
    greet(other_core)

    @pl.when(pipe > 0)
    def _():
        greet({"pipe": pipe - 1})

    @pl.when(pipe < lax.axis_size("pipe") - 1)
    def _():
        greet({"pipe": pipe + 1})

    def put_squares(t, x):
        sums = jnp.sum(x * x, axis=1, keepdims=True)
        sqs[t] = jnp.broadcast_to(sums, (TOK, 128))

    def squares_copy(t):
        return remote(sqs.at[t], sqr.at[t], sq_sem.at[t, 0], sq_sem.at[t, 1], other_core)

    def make_meta():
        row = lax.broadcasted_iota(jnp.int32, (SIDE * SIDE, 128), 0)
        ta = lax.rem(a + row // SIDE, SIDE)
        tb_ = lax.rem(b + offset_of(lax.rem(row, SIDE)), SIDE)
        named = (1 - core) * (ta * SIDE + tb_) + core * (tb_ * SIDE + ta)
        r128 = lax.broadcasted_iota(jnp.int32, (128, 128), 0)
        l128 = lax.broadcasted_iota(jnp.int32, (128, 128), 1)
        earlier = jnp.where((r128 < TOK) & (r128 < lax.rem(l128, TOK)), 1.0, 0.0).astype(BF16)
        for t in range(TICKS):
            ids = jnp.concatenate([ids_ref[t], ids_ref[t]], axis=1)
            prob = jnp.concatenate([prob_ref[t], prob_ref[t]], axis=1)
            gate = prob / jnp.sum(prob, axis=0, keepdims=True)
            member = jnp.zeros((SIDE * SIDE, 128), F32)
            gates = jnp.zeros((SIDE * SIDE, 128), F32)
            for k in range(TOPK):
                hit = named == ids[k : k + 1, :]
                member = member + jnp.where(hit, 1.0, 0.0)
                gates = gates + jnp.where(hit, gate[k : k + 1, :], 0.0)
            slots = jnp.where(member > 0.5, dot(member.astype(BF16), earlier), -1.0)
            ms[:, 16 * t : 16 * t + 8, :] = slots.reshape(SIDE, SIDE, 128)
            ms[:, 16 * t + 8 : 16 * t + 16, :] = gates.reshape(SIDE, SIDE, 128)
        mr[0] = ms[0]

    def build_maps(t):
        row = lax.broadcasted_iota(jnp.int32, (128, 128), 0)
        lane = lax.broadcasted_iota(jnp.int32, (128, 128), 1)
        same = (lax.rem(row, 16) // 8) == (lane // TOK)
        slot = lax.rem(row, 8).astype(F32)
        xrow = lax.broadcasted_iota(jnp.int32, (64, 128), 0)
        xlane = lax.broadcasted_iota(jnp.int32, (64, 128), 1)
        low = lax.broadcasted_iota(jnp.int32, (8, 128), 1) < TOK
        for q in range(4):
            slots = jnp.where(low, mr[2 * q, 16 * t : 16 * t + 8, :], mr[2 * q + 1, 16 * t : 16 * t + 8, :])
            gates = jnp.where(low, mr[2 * q, 16 * t + 8 : 16 * t + 16, :], mr[2 * q + 1, 16 * t + 8 : 16 * t + 16, :])
            wide = jnp.concatenate([jnp.broadcast_to(slots[i : i + 1], (16, 128)) for i in range(8)], axis=0)
            wide_gate = jnp.concatenate([jnp.broadcast_to(gates[i : i + 1], (16, 128)) for i in range(8)], axis=0)
            hit = same & (wide == slot)
            omat[t, q] = jnp.where(hit, 1.0, 0.0).astype(BF16)
            got[t, q] = jnp.where(hit, wide_gate, 0.0).T.astype(BF16)
            wide = jnp.concatenate([jnp.broadcast_to(slots[i : i + 1], (8, 128)) for i in range(8)], axis=0)
            wide_gate = jnp.concatenate([jnp.broadcast_to(gates[i : i + 1], (8, 128)) for i in range(8)], axis=0)
            hit = (lax.rem(xrow, 8) == 2 * q + xlane // TOK) & (wide == 8.0)
            o8[t, :, 128 * q : 128 * q + 128] = jnp.where(hit, 1.0, 0.0).astype(BF16)
            spread_gate = jnp.concatenate([jnp.where(hit, wide_gate, 0.0), jnp.zeros((64, 128), F32)], axis=0)
            g8t[t, q] = spread_gate.T.astype(BF16)

    def pack_extra(rows, ref):
        for p in range(SIDE):
            part = rows[8 * p : 8 * p + 8]
            ref[p] = jnp.concatenate([part[:, :C2], part[:, C2:]], axis=0).astype(BF16)

    def unpack_extra(ref):
        parts = []
        for p in range(SIDE):
            part = ref[p].astype(F32)
            parts.append(jnp.concatenate([part[:8], part[8:]], axis=1))
        return jnp.concatenate(parts, axis=0).astype(BF16)

    x_load.wait()
    put_squares(0, xn[...].astype(F32))
    ids_load.wait()
    prob_load.wait()
    make_meta()
    greeted = 2 * (SIDE - 1) + 1 + jnp.where(pipe > 0, 1, 0) + jnp.where(pipe < lax.axis_size("pipe") - 1, 1, 0)
    pl.semaphore_wait(barrier, greeted)
    squares_copy(0).start()
    for j in range(1, SIDE):
        remote(ms.at[j], mr.at[POS[j]], meta_sem.at[0], meta_sem.at[1], first(j)).start()
    gain_load.wait()

    for t in range(TICKS):
        if t > 0:
            put_squares(t, xn[...].astype(F32))
            squares_copy(t).start()
        squares_copy(t).wait()
        scale = lax.rsqrt((sqs[t] + sqr[t]) / (2.0 * D) + EPS)[:, :1]

        def ring_copy(k, j):
            parent = PARENT[j]
            return remote(
                gb.at[t, k, pl.ds(POS[parent] * TOK, TOK)], gb.at[t, k, pl.ds(POS[j] * TOK, TOK)],
                ring_send.at[t, k], ring_recv.at[t, k, j], first(j - parent),
            )

        for k in range(NC):
            cols = slice(k * C, k * C + C)
            gb[t, k, :TOK] = (xn[:, cols].astype(F32) * scale * gain_ref[:, cols]).astype(BF16)
            for j in CHILDREN[0]:
                ring_copy(k, j).start()
        if t == 0:
            remote(mr.at[pl.ds(1, 7)], mr.at[pl.ds(1, 7)], meta_sem.at[0], meta_sem.at[1], first(1)).wait_recv()
            build_maps(t)

        def main_copy(k, q, i):
            p = POS[i]
            return remote(mb.at[t, k, q, p], rb.at[t, k, q, p], main_send.at[t, k], main_recv.at[t, k, q], second(i))

        def products_copy(q):
            return remote(ps.at[t, q], pr.at[t, q], p_sem.at[t, q, 0], p_sem.at[t, q, 1], other_core)

        def extra_products_copy():
            return remote(pse.at[t], pre.at[t], pe_sem.at[t, 0], pe_sem.at[t, 1], other_core)

        def up_rows(q):
            if t == 0 and q == 0:
                up_load.wait()
            total = None
            for k in range(NC):
                seven = rb.at[t, k, q, pl.ds(1, 7)]
                remote(seven, seven, main_send.at[t, k], main_recv.at[t, k, q], second(1)).wait_recv()
                part = dot(rb[t, k, q].reshape(128, C), wup[k * C : k * C + C])
                total = part if total is None else total + part
            ps[t, q] = total.astype(BF16)
            products_copy(q).start()

        def up_extra():
            total = None
            for k in range(NC):
                seven = rxb.at[t, k, pl.ds(1, 7)]
                remote(seven, seven, ext_sem.at[t, k, 0], ext_sem.at[t, k, 1], second(1)).wait_recv()
                part = dot(unpack_extra(rxb.at[t, k]), wup[k * C : k * C + C])
                total = part if total is None else total + part
            pse[t] = total.astype(BF16)
            extra_products_copy().start()

        for step in range(4):
            for k in range(NC):
                for j in ARRIVALS[step]:
                    ring_copy(k, j).wait_recv()
                    for child in CHILDREN[j]:
                        ring_copy(k, child).start()
            q = step
            for k in range(NC):
                picked = dot(omat[t, q], gb[t, k, 128 * q : 128 * q + 128, :]).astype(BF16).reshape(SIDE, 16, C)
                mb[t, k, q] = picked
                rb[t, k, q, 0] = picked[0]
                for i in FAR_FIRST:
                    main_copy(k, q, i).start()
                if step == 3:
                    pack_extra(dot(o8[t], gb[t, k]), xb.at[t, k])
                    rxb[t, k, 0] = xb[t, k, 0]
                    for i in FAR_FIRST:
                        p = POS[i]
                        remote(xb.at[t, k, p], rxb.at[t, k, p], ext_sem.at[t, k, 0], ext_sem.at[t, k, 1], second(i)).start()
            if step >= 2:
                up_rows(step - 2)
        if t == 0:
            for later in range(1, TICKS):
                build_maps(later)
        up_rows(2)
        up_rows(3)
        up_extra()

        xrow = lax.broadcasted_iota(jnp.int32, (64, 64), 0)
        xlane = lax.broadcasted_iota(jnp.int32, (64, 64), 1)
        swap = jnp.where(xlane == lax.rem(xrow, 8) * 8 + xrow // 8, 1.0, 0.0).astype(BF16)
        for q in range(4):
            products_copy(q).wait_recv()
        extra_products_copy().wait_recv()
        if t == 0:
            down_load.wait()

        def down_extra():
            total = pse[t].astype(F32) + dot(swap, pre[t])
            hidden = (total / (1.0 + jnp.exp(-total))).astype(BF16)
            made = dot(hidden, wdn[...])
            for k in range(NC):
                pack_extra(made[:, k * C : k * C + C], oxb.at[t, k])
                txb[t, k, 0] = oxb[t, k, 0]
                for i in FAR_FIRST:
                    p = POS[i]
                    remote(oxb.at[t, k, p], txb.at[t, k, p], rext_sem.at[t, k, 0], rext_sem.at[t, k, 1], second(-i)).start()

        def down_rows(q):
            parts = []
            for n in range(4):
                block = pr[t, n, 32 * q : 32 * q + 32].astype(F32)
                parts += [block[:8], block[16:24], block[8:16], block[24:]]
            total = ps[t, q].astype(F32) + jnp.concatenate(parts, axis=0)
            hidden = (total / (1.0 + jnp.exp(-total))).astype(BF16)
            for k in range(NC):
                made = dot(hidden, wdn[:, k * C : k * C + C]).astype(BF16).reshape(SIDE, 16, C)
                ob[t, k, q] = made
                tb[t, k, q, 0] = made[0]
                for i in FAR_FIRST:
                    p = POS[i]
                    remote(ob.at[t, k, q, p], tb.at[t, k, q, p], rmain_send.at[t, k], rmain_recv.at[t, k, q], second(-i)).start()

        def back_copy(k, j):
            return remote(
                sb.at[t, k, j], rr.at[t, k, j], back_send.at[t, k], back_recv.at[t, k, j], first(PARENT[j] - j),
            )

        def sum_pair(q):
            for k in range(NC):
                if q == 3:
                    seven = txb.at[t, k, pl.ds(1, 7)]
                    remote(seven, seven, rext_sem.at[t, k, 0], rext_sem.at[t, k, 1], second(1)).wait_recv()
                    te[k] = unpack_extra(txb.at[t, k])
                seven = tb.at[t, k, q, pl.ds(1, 7)]
                remote(seven, seven, rmain_send.at[t, k], rmain_recv.at[t, k, q], second(1)).wait_recv()
                part = dot(got[t, q], tb[t, k, q].reshape(128, C))
                part = part + dot(g8t[t, q][:, :64], te[k])
                for h in (1, 0):
                    j = OFFSETS[2 * q + h]
                    total = part[64 * h : 64 * h + 64]
                    for child in CHILDREN[j]:
                        back_copy(k, child).wait_recv()
                        total = total + rr[t, k, child].astype(F32)
                    if j > 0:
                        sb[t, k, j] = total.astype(BF16)
                        back_copy(k, j).start()
                    else:
                        cols = slice(k * C, k * C + C)
                        y = (xn[:, cols].astype(F32) + total).astype(BF16)
                        if t == TICKS - 1:
                            out_ref[:, cols] = y
                        else:
                            shs[t, k] = y

                            @pl.when(pipe < lax.axis_size("pipe") - 1)
                            def _():
                                remote(shs.at[t, k], shr.at[t, k], sh_send.at[t, k], sh_recv.at[t, k], {"pipe": pipe + 1}).start()

        down_extra()
        down_rows(3)
        down_rows(2)
        sum_pair(3)
        down_rows(1)
        sum_pair(2)
        down_rows(0)
        sum_pair(1)
        sum_pair(0)

        if t < TICKS - 1:
            if t == 0:
                fresh_load.wait()

            @pl.when(pipe > 0)
            def _():
                for k in range(NC):
                    remote(shs.at[t, k], shr.at[t, k], sh_send.at[t, k], sh_recv.at[t, k], {"pipe": pipe - 1}).wait_recv()
                    xn[:, k * C : k * C + C] = shr[t, k]

            @pl.when(pipe == 0)
            def _():
                xn[...] = fresh_ref[t]

    seven = pl.ds(1, 7)

    def sent(ref, semaphore):
        pltpu.make_async_remote_copy(
            src_ref=ref, dst_ref=ref, send_sem=semaphore, recv_sem=meta_sem.at[1],
            device_id=other_core, device_id_type=MESH,
        ).wait_send()

    sent(mr.at[seven], meta_sem.at[0])
    for t in range(TICKS):
        for k in range(NC):
            sent(gb.at[t, k, pl.ds(64, 448)], ring_send.at[t, k])
            sent(mb.at[t, k, :, seven], main_send.at[t, k])
            sent(xb.at[t, k, seven], ext_sem.at[t, k, 0])
            sent(ob.at[t, k, :, seven], rmain_send.at[t, k])
            sent(oxb.at[t, k, seven], rext_sem.at[t, k, 0])
            sent(sb.at[t, k, seven], back_send.at[t, k])
        for q in range(4):
            sent(ps.at[t, q], p_sem.at[t, q, 0])
        sent(pse.at[t], pe_sem.at[t, 0])

    @pl.when(pipe < lax.axis_size("pipe") - 1)
    def _():
        for t in range(TICKS - 1):
            for k in range(NC):
                remote(shs.at[t, k], shr.at[t, k], sh_send.at[t, k], sh_recv.at[t, k], {"pipe": pipe + 1}).wait_send()


def on_device(in_flight, fresh_batch, norm_gain, up_weight, down_weight, expert_ids, route_prob):
    ids = jnp.swapaxes(expert_ids[:, 0], 1, 2)
    prob = jnp.swapaxes(route_prob[:, 0], 1, 2)
    hbm = pl.BlockSpec(memory_space=pl.ANY)
    dma = pltpu.SemaphoreType.DMA
    scratch = [
        pltpu.VMEM((TOK, D), BF16),
        pltpu.VMEM(fresh_batch.shape, BF16),
        pltpu.VMEM((1, D), F32),
        pltpu.VMEM((D, HID), BF16),
        pltpu.VMEM((HID, D), BF16),
        pltpu.VMEM((TICKS, TOPK, TOK), jnp.int32),
        pltpu.VMEM((TICKS, TOPK, TOK), F32),
        pltpu.VMEM((TICKS, NC, 512, C), BF16),
        pltpu.VMEM((TICKS, NC, 4, SIDE, 16, C), BF16),
        pltpu.VMEM((TICKS, NC, SIDE, 16, C2), BF16),
        pltpu.VMEM((TICKS, NC, 4, SIDE, 16, C), BF16),
        pltpu.VMEM((TICKS, NC, SIDE, 16, C2), BF16),
        pltpu.VMEM((TICKS, 4, 128, HID), BF16),
        pltpu.VMEM((TICKS, 4, 128, HID), BF16),
        pltpu.VMEM((TICKS, 64, HID), BF16),
        pltpu.VMEM((TICKS, 64, HID), BF16),
        pltpu.VMEM((TICKS, NC, 4, SIDE, 16, C), BF16),
        pltpu.VMEM((TICKS, NC, SIDE, 16, C2), BF16),
        pltpu.VMEM((TICKS, NC, 4, SIDE, 16, C), BF16),
        pltpu.VMEM((TICKS, NC, SIDE, 16, C2), BF16),
        pltpu.VMEM((NC, 64, C), BF16),
        pltpu.VMEM((TICKS, NC, SIDE, TOK, C), BF16),
        pltpu.VMEM((TICKS, NC, SIDE, TOK, C), BF16),
        pltpu.VMEM((TICKS, TOK, 128), F32),
        pltpu.VMEM((TICKS, TOK, 128), F32),
        pltpu.VMEM((TICKS, NC, TOK, C), BF16),
        pltpu.VMEM((TICKS, NC, TOK, C), BF16),
        pltpu.VMEM((SIDE, 32, 128), F32),
        pltpu.VMEM((SIDE, 32, 128), F32),
        pltpu.VMEM((TICKS, 4, 128, 128), BF16),
        pltpu.VMEM((TICKS, 64, 512), BF16),
        pltpu.VMEM((TICKS, 4, 128, 128), BF16),
        pltpu.VMEM((TICKS, 4, 128, 128), BF16),
        dma((7,)), dma((2,)), dma((TICKS, 2)), dma((TICKS, NC)), dma((TICKS, NC)),
        dma((TICKS, NC)), dma((TICKS, NC, SIDE)), dma((TICKS, NC)), dma((TICKS, NC, 4)), dma((TICKS, NC, 2)),
        dma((TICKS, 4, 2)), dma((TICKS, 2)), dma((TICKS, NC)), dma((TICKS, NC, 4)), dma((TICKS, NC, 2)),
        dma((TICKS, NC)), dma((TICKS, NC, SIDE)),
    ]
    y = pl.pallas_call(
        kernel,
        name="window",
        out_shape=jax.ShapeDtypeStruct((TOK, D), BF16),
        in_specs=[hbm] * 7,
        out_specs=pl.BlockSpec(memory_space=pltpu.VMEM),
        scratch_shapes=scratch,
        compiler_params=pltpu.CompilerParams(
            collective_id=0, has_side_effects=True, vmem_limit_bytes=62 * 2**20
        ),
    )(in_flight[0], fresh_batch, norm_gain, up_weight[0, 0], down_weight[0, 0], ids, prob)
    return y[None]


def solution(mesh):
    placed = (
        P("pipe", "expert", "tensor"),
        P(None, "expert", "tensor"),
        P("pipe", "tensor"),
        P("pipe", "expert", "tensor", None),
        P("pipe", "expert", None, "tensor"),
        P(None, "pipe", "expert", None),
        P(None, "pipe", "expert", None),
    )
    return jax.shard_map(
        on_device,
        mesh=mesh,
        in_specs=placed,
        out_specs=P("pipe", "expert", "tensor"),
        check_vma=False,
    )
```

```python
import functools
import jax
import jax.numpy as jnp
from jax import lax
import jax.experimental.pallas as pl
import jax.experimental.pallas.tpu as pltpu
from jax.sharding import PartitionSpec as P

EPS = 1e-06
MESH = pl.DeviceIdType.MESH
F32 = jnp.float32
BF16 = jnp.bfloat16

SIDE = 8
TOK = 64
TOPK = 8
D = 1024
HID = 768
NC = 2
C = D // NC
C2 = C // 2
TICKS = 2

OFFSETS = (0, 1, 7, 2, 6, 3, 5, 4)
POS = {j: p for p, j in enumerate(OFFSETS)}
PARENT = {1: 0, 7: 0, 2: 0, 6: 0, 3: 2, 5: 6, 4: 3}
CHILDREN = {j: tuple(c for c in PARENT if PARENT[c] == j) for j in range(SIDE)}
ARRIVALS = ((1, 7), (2, 6), (3, 5), (4,))
FAR_FIRST = (4, 3, 5, 2, 6, 1, 7)


def offset_of(position):
    odd = lax.rem(position, 2) == 1
    return jnp.where(odd, (position + 1) // 2, lax.rem(SIDE - position // 2, SIDE))


def dot(a, b):
    return jnp.dot(a, b, preferred_element_type=F32)


def kernel(
    x_hbm, fresh_hbm, gain_hbm, up_hbm, down_hbm, ids_hbm, prob_hbm, out_ref,
    xn, fresh_ref, gain_ref, wup, wdn, ids_ref, prob_ref,
    gb, mb, xb, rb, rxb, ps, pr, pse, pre, ob, oxb, tb, txb, te, sb, rr,
    sqs, sqr, sqy, shs, shr, ms, mr, omat, o8, got, g8t,
    load_sem, meta_sem, sq_sem, sqy_send, sqy_recv, sh_send, sh_recv, ring_send, ring_recv, main_send, main_recv, ext_sem,
    p_sem, pe_sem, rmain_send, rmain_recv, rext_sem, back_send, back_recv,
):
    core = lax.axis_index("tensor")
    expert = lax.axis_index("expert")
    pipe = lax.axis_index("pipe")
    ez, ey = expert // SIDE, lax.rem(expert, SIDE)
    a = (1 - core) * ez + core * ey
    b = (1 - core) * ey + core * ez

    def device_at(da, db):
        ta, tb_ = lax.rem(a + da + SIDE, SIDE), lax.rem(b + db + SIDE, SIDE)
        return {"expert": (1 - core) * (ta * SIDE + tb_) + core * (tb_ * SIDE + ta)}

    def first(da):
        return device_at(da, 0)

    def second(db):
        return device_at(0, db)

    def remote(src, dst, send, recv, device):
        return pltpu.make_async_remote_copy(
            src_ref=src, dst_ref=dst, send_sem=send, recv_sem=recv,
            device_id=device, device_id_type=MESH,
        )

    loads = [
        pltpu.make_async_copy(source, held, load_sem.at[n])
        for n, (source, held) in enumerate((
            (x_hbm, xn), (ids_hbm, ids_ref), (prob_hbm, prob_ref), (gain_hbm, gain_ref),
            (fresh_hbm, fresh_ref), (up_hbm, wup), (down_hbm, wdn),
        ))
    ]
    for load in loads:
        load.start()
    x_load, ids_load, prob_load, gain_load, fresh_load, up_load, down_load = loads

    barrier = pltpu.get_barrier_semaphore()
    other_core = {"tensor": 1 - core}

    def greet(device):
        pl.semaphore_signal(barrier, inc=1, device_id=device, device_id_type=MESH)

    for d in range(1, SIDE):
        greet(first(d))
        greet(second(d))
    greet(other_core)

    @pl.when(pipe > 0)
    def _():
        greet({"pipe": pipe - 1})
        greet({"pipe": pipe - 1, "tensor": 1 - core})

    @pl.when(pipe < lax.axis_size("pipe") - 1)
    def _():
        greet({"pipe": pipe + 1})
        greet({"pipe": pipe + 1, "tensor": 1 - core})

    def put_squares(t, x):
        sums = jnp.sum(x * x, axis=1, keepdims=True)
        sqs[t] = jnp.broadcast_to(sums, (TOK, 128))

    def squares_copy(t):
        return remote(sqs.at[t], sqr.at[t], sq_sem.at[t, 0], sq_sem.at[t, 1], other_core)

    def passed_squares(t, by):
        return (
            remote(sqy.at[t], sqs.at[t], sqy_send.at[t, 0], sqy_recv.at[t, 0], {"pipe": pipe + by}),
            remote(sqy.at[t], sqr.at[t], sqy_send.at[t, 1], sqy_recv.at[t, 1], {"pipe": pipe + by, "tensor": 1 - core}),
        )

    def make_meta():
        row = lax.broadcasted_iota(jnp.int32, (SIDE * SIDE, 128), 0)
        ta = lax.rem(a + row // SIDE, SIDE)
        tb_ = lax.rem(b + offset_of(lax.rem(row, SIDE)), SIDE)
        named = (1 - core) * (ta * SIDE + tb_) + core * (tb_ * SIDE + ta)
        r128 = lax.broadcasted_iota(jnp.int32, (128, 128), 0)
        l128 = lax.broadcasted_iota(jnp.int32, (128, 128), 1)
        earlier = jnp.where((r128 < TOK) & (r128 < lax.rem(l128, TOK)), 1.0, 0.0).astype(BF16)
        for t in range(TICKS):
            ids = jnp.concatenate([ids_ref[t], ids_ref[t]], axis=1)
            prob = jnp.concatenate([prob_ref[t], prob_ref[t]], axis=1)
            gate = prob / jnp.sum(prob, axis=0, keepdims=True)
            member = jnp.zeros((SIDE * SIDE, 128), F32)
            gates = jnp.zeros((SIDE * SIDE, 128), F32)
            for k in range(TOPK):
                hit = named == ids[k : k + 1, :]
                member = member + jnp.where(hit, 1.0, 0.0)
                gates = gates + jnp.where(hit, gate[k : k + 1, :], 0.0)
            slots = jnp.where(member > 0.5, dot(member.astype(BF16), earlier), -1.0)
            ms[:, 16 * t : 16 * t + 8, :] = slots.reshape(SIDE, SIDE, 128)
            ms[:, 16 * t + 8 : 16 * t + 16, :] = gates.reshape(SIDE, SIDE, 128)
        mr[0] = ms[0]

    def build_maps(t, back):
        row = lax.broadcasted_iota(jnp.int32, (128, 128), 0)
        lane = lax.broadcasted_iota(jnp.int32, (128, 128), 1)
        same = (lax.rem(row, 16) // 8) == (lane // TOK)
        slot = lax.rem(row, 8).astype(F32)
        xrow = lax.broadcasted_iota(jnp.int32, (64, 128), 0)
        xlane = lax.broadcasted_iota(jnp.int32, (64, 128), 1)
        low = lax.broadcasted_iota(jnp.int32, (8, 128), 1) < TOK

        def widen(rows, times):
            return jnp.concatenate([jnp.broadcast_to(rows[i : i + 1], (times, 128)) for i in range(8)], axis=0)

        for q in range(4):
            slots = jnp.where(low, mr[2 * q, 16 * t : 16 * t + 8, :], mr[2 * q + 1, 16 * t : 16 * t + 8, :])
            hit = same & (widen(slots, 16) == slot)
            extra_hit = (lax.rem(xrow, 8) == 2 * q + xlane // TOK) & (widen(slots, 8) == 8.0)
            if back:
                gates = jnp.where(low, mr[2 * q, 16 * t + 8 : 16 * t + 16, :], mr[2 * q + 1, 16 * t + 8 : 16 * t + 16, :])
                got[t, q] = jnp.where(hit, widen(gates, 16), 0.0).T.astype(BF16)
                spread_gate = jnp.concatenate([jnp.where(extra_hit, widen(gates, 8), 0.0), jnp.zeros((64, 128), F32)], axis=0)
                g8t[t, q] = spread_gate.T.astype(BF16)
            else:
                omat[t, q] = jnp.where(hit, 1.0, 0.0).astype(BF16)
                o8[t, :, 128 * q : 128 * q + 128] = jnp.where(extra_hit, 1.0, 0.0).astype(BF16)

    def pack_extra(rows, ref):
        for p in range(SIDE):
            part = rows[8 * p : 8 * p + 8]
            ref[p] = jnp.concatenate([part[:, :C2], part[:, C2:]], axis=0).astype(BF16)

    def unpack_extra(ref):
        parts = []
        for p in range(SIDE):
            part = ref[p].astype(F32)
            parts.append(jnp.concatenate([part[:8], part[8:]], axis=1))
        return jnp.concatenate(parts, axis=0).astype(BF16)

    x_load.wait()
    put_squares(0, xn[...].astype(F32))
    ids_load.wait()
    prob_load.wait()
    make_meta()
    greeted = 2 * (SIDE - 1) + 1 + jnp.where(pipe > 0, 2, 0) + jnp.where(pipe < lax.axis_size("pipe") - 1, 2, 0)
    pl.semaphore_wait(barrier, greeted)
    squares_copy(0).start()
    for j in range(1, SIDE):
        remote(ms.at[j], mr.at[POS[j]], meta_sem.at[0], meta_sem.at[1], first(j)).start()
    gain_load.wait()

    for t in range(TICKS):
        if t == 0:
            squares_copy(t).wait()
        else:
            @pl.when(pipe > 0)
            def _():
                for copy in passed_squares(t, -1):
                    copy.wait_recv()

        scale = lax.rsqrt((sqs[t] + sqr[t]) / (2.0 * D) + EPS)[:, :1]

        def ring_copy(k, j):
            parent = PARENT[j]
            return remote(
                gb.at[t, k, pl.ds(POS[parent] * TOK, TOK)], gb.at[t, k, pl.ds(POS[j] * TOK, TOK)],
                ring_send.at[t, k], ring_recv.at[t, k, j], first(j - parent),
            )

        for k in range(NC):
            cols = slice(k * C, k * C + C)
            gb[t, k, :TOK] = (xn[:, cols].astype(F32) * scale * gain_ref[:, cols]).astype(BF16)
            for j in CHILDREN[0]:
                ring_copy(k, j).start()
        if t == 0:
            remote(mr.at[pl.ds(1, 7)], mr.at[pl.ds(1, 7)], meta_sem.at[0], meta_sem.at[1], first(1)).wait_recv()
            build_maps(0, False)

        def main_copy(k, q, i):
            p = POS[i]
            return remote(mb.at[t, k, q, p], rb.at[t, k, q, p], main_send.at[t, k], main_recv.at[t, k, q], second(i))

        def products_copy(q):
            return remote(ps.at[t, q], pr.at[t, q], p_sem.at[t, q, 0], p_sem.at[t, q, 1], other_core)

        def extra_products_copy():
            return remote(pse.at[t], pre.at[t], pe_sem.at[t, 0], pe_sem.at[t, 1], other_core)

        def up_rows(q):
            if t == 0 and q == 0:
                up_load.wait()
            total = None
            for k in range(NC):
                seven = rb.at[t, k, q, pl.ds(1, 7)]
                remote(seven, seven, main_send.at[t, k], main_recv.at[t, k, q], second(1)).wait_recv()
                part = dot(rb[t, k, q].reshape(128, C), wup[k * C : k * C + C])
                total = part if total is None else total + part
            ps[t, q] = total.astype(BF16)
            products_copy(q).start()

        def up_extra():
            total = None
            for k in range(NC):
                seven = rxb.at[t, k, pl.ds(1, 7)]
                remote(seven, seven, ext_sem.at[t, k, 0], ext_sem.at[t, k, 1], second(1)).wait_recv()
                part = dot(unpack_extra(rxb.at[t, k]), wup[k * C : k * C + C])
                total = part if total is None else total + part
            pse[t] = total.astype(BF16)
            extra_products_copy().start()

        for step in range(4):
            for k in range(NC):
                for j in ARRIVALS[step]:
                    ring_copy(k, j).wait_recv()
                    for child in CHILDREN[j]:
                        ring_copy(k, child).start()
            q = step
            for k in range(NC):
                picked = dot(omat[t, q], gb[t, k, 128 * q : 128 * q + 128, :]).astype(BF16).reshape(SIDE, 16, C)
                mb[t, k, q] = picked
                rb[t, k, q, 0] = picked[0]
                for i in FAR_FIRST:
                    main_copy(k, q, i).start()
                if step == 3:
                    pack_extra(dot(o8[t], gb[t, k]), xb.at[t, k])
                    rxb[t, k, 0] = xb[t, k, 0]
                    for i in FAR_FIRST:
                        p = POS[i]
                        remote(xb.at[t, k, p], rxb.at[t, k, p], ext_sem.at[t, k, 0], ext_sem.at[t, k, 1], second(i)).start()
            if step >= 2:
                up_rows(step - 2)
        if t == 0:
            build_maps(0, True)
            for later in range(1, TICKS):
                build_maps(later, False)
                build_maps(later, True)
        up_rows(2)
        up_rows(3)
        up_extra()

        xrow = lax.broadcasted_iota(jnp.int32, (64, 64), 0)
        xlane = lax.broadcasted_iota(jnp.int32, (64, 64), 1)
        swap = jnp.where(xlane == lax.rem(xrow, 8) * 8 + xrow // 8, 1.0, 0.0).astype(BF16)
        for q in range(4):
            products_copy(q).wait_recv()
        extra_products_copy().wait_recv()
        if t == 0:
            down_load.wait()

        def down_extra():
            total = pse[t].astype(F32) + dot(swap, pre[t])
            hidden = (total / (1.0 + jnp.exp(-total))).astype(BF16)
            made = dot(hidden, wdn[...])
            for k in range(NC):
                pack_extra(made[:, k * C : k * C + C], oxb.at[t, k])
                txb[t, k, 0] = oxb[t, k, 0]
                for i in FAR_FIRST:
                    p = POS[i]
                    remote(oxb.at[t, k, p], txb.at[t, k, p], rext_sem.at[t, k, 0], rext_sem.at[t, k, 1], second(-i)).start()

        def down_rows(q):
            parts = []
            for n in range(4):
                block = pr[t, n, 32 * q : 32 * q + 32].astype(F32)
                parts += [block[:8], block[16:24], block[8:16], block[24:]]
            total = ps[t, q].astype(F32) + jnp.concatenate(parts, axis=0)
            hidden = (total / (1.0 + jnp.exp(-total))).astype(BF16)
            for k in range(NC):
                made = dot(hidden, wdn[:, k * C : k * C + C]).astype(BF16).reshape(SIDE, 16, C)
                ob[t, k, q] = made
                tb[t, k, q, 0] = made[0]
                for i in FAR_FIRST:
                    p = POS[i]
                    remote(ob.at[t, k, q, p], tb.at[t, k, q, p], rmain_send.at[t, k], rmain_recv.at[t, k, q], second(-i)).start()

        def back_copy(k, j):
            return remote(
                sb.at[t, k, j], rr.at[t, k, j], back_send.at[t, k], back_recv.at[t, k, j], first(PARENT[j] - j),
            )

        def sum_pair(q):
            squares = jnp.zeros((TOK, 1), F32)
            for k in range(NC):
                if q == 3:
                    seven = txb.at[t, k, pl.ds(1, 7)]
                    remote(seven, seven, rext_sem.at[t, k, 0], rext_sem.at[t, k, 1], second(1)).wait_recv()
                    te[k] = unpack_extra(txb.at[t, k])
                seven = tb.at[t, k, q, pl.ds(1, 7)]
                remote(seven, seven, rmain_send.at[t, k], rmain_recv.at[t, k, q], second(1)).wait_recv()
                part = dot(got[t, q], tb[t, k, q].reshape(128, C))
                part = part + dot(g8t[t, q][:, :64], te[k])
                for h in (1, 0):
                    j = OFFSETS[2 * q + h]
                    total = part[64 * h : 64 * h + 64]
                    for child in CHILDREN[j]:
                        back_copy(k, child).wait_recv()
                        total = total + rr[t, k, child].astype(F32)
                    if j > 0:
                        sb[t, k, j] = total.astype(BF16)
                        back_copy(k, j).start()
                    else:
                        cols = slice(k * C, k * C + C)
                        y = (xn[:, cols].astype(F32) + total).astype(BF16)
                        if t == TICKS - 1:
                            out_ref[:, cols] = y
                        else:
                            shs[t, k] = y

                            @pl.when(pipe < lax.axis_size("pipe") - 1)
                            def _():
                                remote(shs.at[t, k], shr.at[t, k], sh_send.at[t, k], sh_recv.at[t, k], {"pipe": pipe + 1}).start()

                            squares = squares + jnp.sum(y.astype(F32) * y.astype(F32), axis=1, keepdims=True)
                            if k == NC - 1:
                                sqy[t + 1] = jnp.broadcast_to(squares, (TOK, 128))

                                @pl.when(pipe < lax.axis_size("pipe") - 1)
                                def _():
                                    for copy in passed_squares(t + 1, 1):
                                        copy.start()

        down_extra()
        down_rows(3)
        down_rows(2)
        sum_pair(3)
        down_rows(1)
        sum_pair(2)
        down_rows(0)
        sum_pair(1)
        sum_pair(0)

        if t < TICKS - 1:
            if t == 0:
                fresh_load.wait()

            @pl.when(pipe > 0)
            def _():
                for k in range(NC):
                    remote(shs.at[t, k], shr.at[t, k], sh_send.at[t, k], sh_recv.at[t, k], {"pipe": pipe - 1}).wait_recv()
                    xn[:, k * C : k * C + C] = shr[t, k]

            @pl.when(pipe == 0)
            def _():
                xn[...] = fresh_ref[t]
                put_squares(t + 1, fresh_ref[t].astype(F32))
                squares_copy(t + 1).start()
                squares_copy(t + 1).wait()

    seven = pl.ds(1, 7)

    def sent(ref, semaphore):
        pltpu.make_async_remote_copy(
            src_ref=ref, dst_ref=ref, send_sem=semaphore, recv_sem=meta_sem.at[1],
            device_id=other_core, device_id_type=MESH,
        ).wait_send()

    sent(mr.at[seven], meta_sem.at[0])
    for t in range(TICKS):
        for k in range(NC):
            sent(gb.at[t, k, pl.ds(64, 448)], ring_send.at[t, k])
            sent(mb.at[t, k, :, seven], main_send.at[t, k])
            sent(xb.at[t, k, seven], ext_sem.at[t, k, 0])
            sent(ob.at[t, k, :, seven], rmain_send.at[t, k])
            sent(oxb.at[t, k, seven], rext_sem.at[t, k, 0])
            sent(sb.at[t, k, seven], back_send.at[t, k])
        for q in range(4):
            sent(ps.at[t, q], p_sem.at[t, q, 0])
        sent(pse.at[t], pe_sem.at[t, 0])

    @pl.when(pipe < lax.axis_size("pipe") - 1)
    def _():
        for t in range(TICKS - 1):
            for copy in passed_squares(t + 1, 1):
                copy.wait_send()
            for k in range(NC):
                remote(shs.at[t, k], shr.at[t, k], sh_send.at[t, k], sh_recv.at[t, k], {"pipe": pipe + 1}).wait_send()


def on_device(in_flight, fresh_batch, norm_gain, up_weight, down_weight, expert_ids, route_prob):
    ids = jnp.swapaxes(expert_ids[:, 0], 1, 2)
    prob = jnp.swapaxes(route_prob[:, 0], 1, 2)
    hbm = pl.BlockSpec(memory_space=pl.ANY)
    dma = pltpu.SemaphoreType.DMA
    scratch = [
        pltpu.VMEM((TOK, D), BF16),
        pltpu.VMEM(fresh_batch.shape, BF16),
        pltpu.VMEM((1, D), F32),
        pltpu.VMEM((D, HID), BF16),
        pltpu.VMEM((HID, D), BF16),
        pltpu.VMEM((TICKS, TOPK, TOK), jnp.int32),
        pltpu.VMEM((TICKS, TOPK, TOK), F32),
        pltpu.VMEM((TICKS, NC, 512, C), BF16),
        pltpu.VMEM((TICKS, NC, 4, SIDE, 16, C), BF16),
        pltpu.VMEM((TICKS, NC, SIDE, 16, C2), BF16),
        pltpu.VMEM((TICKS, NC, 4, SIDE, 16, C), BF16),
        pltpu.VMEM((TICKS, NC, SIDE, 16, C2), BF16),
        pltpu.VMEM((TICKS, 4, 128, HID), BF16),
        pltpu.VMEM((TICKS, 4, 128, HID), BF16),
        pltpu.VMEM((TICKS, 64, HID), BF16),
        pltpu.VMEM((TICKS, 64, HID), BF16),
        pltpu.VMEM((TICKS, NC, 4, SIDE, 16, C), BF16),
        pltpu.VMEM((TICKS, NC, SIDE, 16, C2), BF16),
        pltpu.VMEM((TICKS, NC, 4, SIDE, 16, C), BF16),
        pltpu.VMEM((TICKS, NC, SIDE, 16, C2), BF16),
        pltpu.VMEM((NC, 64, C), BF16),
        pltpu.VMEM((TICKS, NC, SIDE, TOK, C), BF16),
        pltpu.VMEM((TICKS, NC, SIDE, TOK, C), BF16),
        pltpu.VMEM((TICKS, TOK, 128), F32),
        pltpu.VMEM((TICKS, TOK, 128), F32),
        pltpu.VMEM((TICKS, TOK, 128), F32),
        pltpu.VMEM((TICKS, NC, TOK, C), BF16),
        pltpu.VMEM((TICKS, NC, TOK, C), BF16),
        pltpu.VMEM((SIDE, 32, 128), F32),
        pltpu.VMEM((SIDE, 32, 128), F32),
        pltpu.VMEM((TICKS, 4, 128, 128), BF16),
        pltpu.VMEM((TICKS, 64, 512), BF16),
        pltpu.VMEM((TICKS, 4, 128, 128), BF16),
        pltpu.VMEM((TICKS, 4, 128, 128), BF16),
        dma((7,)), dma((2,)), dma((TICKS, 2)), dma((TICKS, 2)), dma((TICKS, 2)), dma((TICKS, NC)), dma((TICKS, NC)),
        dma((TICKS, NC)), dma((TICKS, NC, SIDE)), dma((TICKS, NC)), dma((TICKS, NC, 4)), dma((TICKS, NC, 2)),
        dma((TICKS, 4, 2)), dma((TICKS, 2)), dma((TICKS, NC)), dma((TICKS, NC, 4)), dma((TICKS, NC, 2)),
        dma((TICKS, NC)), dma((TICKS, NC, SIDE)),
    ]
    y = pl.pallas_call(
        kernel,
        name="window",
        out_shape=jax.ShapeDtypeStruct((TOK, D), BF16),
        in_specs=[hbm] * 7,
        out_specs=pl.BlockSpec(memory_space=pltpu.VMEM),
        scratch_shapes=scratch,
        compiler_params=pltpu.CompilerParams(
            collective_id=0, has_side_effects=True, vmem_limit_bytes=62 * 2**20
        ),
    )(in_flight[0], fresh_batch, norm_gain, up_weight[0, 0], down_weight[0, 0], ids, prob)
    return y[None]


def solution(mesh):
    placed = (
        P("pipe", "expert", "tensor"),
        P(None, "expert", "tensor"),
        P("pipe", "tensor"),
        P("pipe", "expert", "tensor", None),
        P("pipe", "expert", None, "tensor"),
        P(None, "pipe", "expert", None),
        P(None, "pipe", "expert", None),
    )
    return jax.shard_map(
        on_device,
        mesh=mesh,
        in_specs=placed,
        out_specs=P("pipe", "expert", "tensor"),
        check_vma=False,
    )
```

```python
import functools
import jax
import jax.numpy as jnp
from jax import lax
import jax.experimental.pallas as pl
import jax.experimental.pallas.tpu as pltpu
from jax.sharding import PartitionSpec as P

EPS = 1e-06
MESH = pl.DeviceIdType.MESH
F32 = jnp.float32
BF16 = jnp.bfloat16

SIDE = 8
TOK = 64
TOPK = 8
D = 1024
HID = 768
NC = 2
C = D // NC
C2 = C // 2
TICKS = 2

OFFSETS = (0, 1, 7, 2, 6, 3, 5, 4)
POS = {j: p for p, j in enumerate(OFFSETS)}
PARENT = {1: 0, 7: 0, 2: 0, 6: 0, 3: 2, 5: 6, 4: 3}
CHILDREN = {j: tuple(c for c in PARENT if PARENT[c] == j) for j in range(SIDE)}
ARRIVALS = ((1, 7), (2, 6), (3, 5), (4,))
FAR_FIRST = (4, 3, 5, 2, 6, 1, 7)


def offset_of(position):
    odd = lax.rem(position, 2) == 1
    return jnp.where(odd, (position + 1) // 2, lax.rem(SIDE - position // 2, SIDE))


def silu(v):
    half = 0.5 * v
    return half + half * jnp.tanh(half)


def dot(a, b):
    return jnp.dot(a, b, preferred_element_type=F32)


def kernel(
    x_hbm, fresh_hbm, gain_hbm, up_hbm, down_hbm, ids_hbm, prob_hbm, out_ref,
    xn, fresh_ref, gain_ref, wup, wdn, ids_ref, prob_ref,
    gb, mb, xb, rb, rxb, ps, pr, pse, pre, ob, oxb, tb, txb, te, sb, rr,
    sqs, sqr, sqy, shs, shr, ms, mr, omat, o8, got, g8t,
    load_sem, meta_sem, sq_sem, sqy_send, sqy_recv, sh_send, sh_recv, ring_send, ring_recv, main_send, main_recv, ext_sem,
    p_sem, pe_sem, rmain_send, rmain_recv, rext_sem, back_send, back_recv,
):
    core = lax.axis_index("tensor")
    expert = lax.axis_index("expert")
    pipe = lax.axis_index("pipe")
    ez, ey = expert // SIDE, lax.rem(expert, SIDE)
    a = (1 - core) * ez + core * ey
    b = (1 - core) * ey + core * ez

    def device_at(da, db):
        ta, tb_ = lax.rem(a + da + SIDE, SIDE), lax.rem(b + db + SIDE, SIDE)
        return {"expert": (1 - core) * (ta * SIDE + tb_) + core * (tb_ * SIDE + ta)}

    def first(da):
        return device_at(da, 0)

    def second(db):
        return device_at(0, db)

    def remote(src, dst, send, recv, device):
        return pltpu.make_async_remote_copy(
            src_ref=src, dst_ref=dst, send_sem=send, recv_sem=recv,
            device_id=device, device_id_type=MESH,
        )

    loads = [
        pltpu.make_async_copy(source, held, load_sem.at[n])
        for n, (source, held) in enumerate((
            (x_hbm, xn), (ids_hbm, ids_ref), (prob_hbm, prob_ref), (gain_hbm, gain_ref),
            (fresh_hbm, fresh_ref), (up_hbm, wup), (down_hbm, wdn),
        ))
    ]
    for load in loads:
        load.start()
    x_load, ids_load, prob_load, gain_load, fresh_load, up_load, down_load = loads

    barrier = pltpu.get_barrier_semaphore()
    other_core = {"tensor": 1 - core}

    def greet(device):
        pl.semaphore_signal(barrier, inc=1, device_id=device, device_id_type=MESH)

    for d in range(1, SIDE):
        greet(first(d))
        greet(second(d))
    greet(other_core)

    @pl.when(pipe > 0)
    def _():
        greet({"pipe": pipe - 1})
        greet({"pipe": pipe - 1, "tensor": 1 - core})

    @pl.when(pipe < lax.axis_size("pipe") - 1)
    def _():
        greet({"pipe": pipe + 1})
        greet({"pipe": pipe + 1, "tensor": 1 - core})

    def put_squares(t, x):
        sums = jnp.sum(x * x, axis=1, keepdims=True)
        sqs[t] = jnp.broadcast_to(sums, (TOK, 128))

    def squares_copy(t):
        return remote(sqs.at[t], sqr.at[t], sq_sem.at[t, 0], sq_sem.at[t, 1], other_core)

    def passed_squares(t, by):
        return (
            remote(sqy.at[t], sqs.at[t], sqy_send.at[t, 0], sqy_recv.at[t, 0], {"pipe": pipe + by}),
            remote(sqy.at[t], sqr.at[t], sqy_send.at[t, 1], sqy_recv.at[t, 1], {"pipe": pipe + by, "tensor": 1 - core}),
        )

    def make_meta():
        row = lax.broadcasted_iota(jnp.int32, (SIDE * SIDE, 128), 0)
        ta = lax.rem(a + row // SIDE, SIDE)
        tb_ = lax.rem(b + offset_of(lax.rem(row, SIDE)), SIDE)
        named = (1 - core) * (ta * SIDE + tb_) + core * (tb_ * SIDE + ta)
        r128 = lax.broadcasted_iota(jnp.int32, (128, 128), 0)
        l128 = lax.broadcasted_iota(jnp.int32, (128, 128), 1)
        earlier = jnp.where((r128 < TOK) & (r128 < lax.rem(l128, TOK)), 1.0, 0.0).astype(BF16)
        for t in range(TICKS):
            ids = jnp.concatenate([ids_ref[t], ids_ref[t]], axis=1)
            prob = jnp.concatenate([prob_ref[t], prob_ref[t]], axis=1)
            gate = prob / jnp.sum(prob, axis=0, keepdims=True)
            member = jnp.zeros((SIDE * SIDE, 128), F32)
            gates = jnp.zeros((SIDE * SIDE, 128), F32)
            for k in range(TOPK):
                hit = named == ids[k : k + 1, :]
                member = member + jnp.where(hit, 1.0, 0.0)
                gates = gates + jnp.where(hit, gate[k : k + 1, :], 0.0)
            slots = jnp.where(member > 0.5, dot(member.astype(BF16), earlier), -1.0)
            ms[:, 16 * t : 16 * t + 8, :] = slots.reshape(SIDE, SIDE, 128)
            ms[:, 16 * t + 8 : 16 * t + 16, :] = gates.reshape(SIDE, SIDE, 128)
        mr[0] = ms[0]

    def build_maps(t, back):
        row = lax.broadcasted_iota(jnp.int32, (128, 128), 0)
        lane = lax.broadcasted_iota(jnp.int32, (128, 128), 1)
        same = (lax.rem(row, 16) // 8) == (lane // TOK)
        slot = lax.rem(row, 8).astype(F32)
        xrow = lax.broadcasted_iota(jnp.int32, (64, 128), 0)
        xlane = lax.broadcasted_iota(jnp.int32, (64, 128), 1)
        low = lax.broadcasted_iota(jnp.int32, (8, 128), 1) < TOK

        def widen(rows, times):
            return jnp.concatenate([jnp.broadcast_to(rows[i : i + 1], (times, 128)) for i in range(8)], axis=0)

        for q in range(4):
            slots = jnp.where(low, mr[2 * q, 16 * t : 16 * t + 8, :], mr[2 * q + 1, 16 * t : 16 * t + 8, :])
            hit = same & (widen(slots, 16) == slot)
            extra_hit = (lax.rem(xrow, 8) == 2 * q + xlane // TOK) & (widen(slots, 8) == 8.0)
            if back:
                gates = jnp.where(low, mr[2 * q, 16 * t + 8 : 16 * t + 16, :], mr[2 * q + 1, 16 * t + 8 : 16 * t + 16, :])
                got[t, q] = jnp.where(hit, widen(gates, 16), 0.0).T.astype(BF16)
                spread_gate = jnp.concatenate([jnp.where(extra_hit, widen(gates, 8), 0.0), jnp.zeros((64, 128), F32)], axis=0)
                g8t[t, q] = spread_gate.T.astype(BF16)
            else:
                omat[t, q] = jnp.where(hit, 1.0, 0.0).astype(BF16)
                o8[t, :, 128 * q : 128 * q + 128] = jnp.where(extra_hit, 1.0, 0.0).astype(BF16)

    def pack_extra(rows, ref):
        for p in range(SIDE):
            part = rows[8 * p : 8 * p + 8]
            ref[p] = jnp.concatenate([part[:, :C2], part[:, C2:]], axis=0).astype(BF16)

    def unpack_extra(ref):
        parts = []
        for p in range(SIDE):
            part = ref[p].astype(F32)
            parts.append(jnp.concatenate([part[:8], part[8:]], axis=1))
        return jnp.concatenate(parts, axis=0).astype(BF16)

    x_load.wait()
    put_squares(0, xn[...].astype(F32))
    ids_load.wait()
    prob_load.wait()
    make_meta()
    greeted = 2 * (SIDE - 1) + 1 + jnp.where(pipe > 0, 2, 0) + jnp.where(pipe < lax.axis_size("pipe") - 1, 2, 0)
    pl.semaphore_wait(barrier, greeted)
    squares_copy(0).start()
    for j in range(1, SIDE):
        remote(ms.at[j], mr.at[POS[j]], meta_sem.at[0], meta_sem.at[1], first(j)).start()
    gain_load.wait()

    for t in range(TICKS):
        if t == 0:
            squares_copy(t).wait()
        else:
            @pl.when(pipe > 0)
            def _():
                for copy in passed_squares(t, -1):
                    copy.wait_recv()

        scale = lax.rsqrt((sqs[t] + sqr[t]) / (2.0 * D) + EPS)[:, :1]

        def ring_copy(k, j):
            parent = PARENT[j]
            return remote(
                gb.at[t, k, pl.ds(POS[parent] * TOK, TOK)], gb.at[t, k, pl.ds(POS[j] * TOK, TOK)],
                ring_send.at[t, k], ring_recv.at[t, k, j], first(j - parent),
            )

        for k in range(NC):
            cols = slice(k * C, k * C + C)
            gb[t, k, :TOK] = (xn[:, cols].astype(F32) * scale * gain_ref[:, cols]).astype(BF16)
            for j in CHILDREN[0]:
                ring_copy(k, j).start()
        if t == 0:
            remote(mr.at[pl.ds(1, 7)], mr.at[pl.ds(1, 7)], meta_sem.at[0], meta_sem.at[1], first(1)).wait_recv()
            build_maps(0, False)

        def main_copy(k, q, i):
            p = POS[i]
            return remote(mb.at[t, k, q, p], rb.at[t, k, q, p], main_send.at[t, k], main_recv.at[t, k, q], second(i))

        def products_copy(q):
            return remote(ps.at[t, q], pr.at[t, q], p_sem.at[t, q, 0], p_sem.at[t, q, 1], other_core)

        def extra_products_copy():
            return remote(pse.at[t], pre.at[t], pe_sem.at[t, 0], pe_sem.at[t, 1], other_core)

        def up_rows(q):
            if t == 0 and q == 0:
                up_load.wait()
            total = None
            for k in range(NC):
                seven = rb.at[t, k, q, pl.ds(1, 7)]
                remote(seven, seven, main_send.at[t, k], main_recv.at[t, k, q], second(1)).wait_recv()
                part = dot(rb[t, k, q].reshape(128, C), wup[k * C : k * C + C])
                total = part if total is None else total + part
            ps[t, q] = total.astype(BF16)
            products_copy(q).start()

        def up_extra():
            total = None
            for k in range(NC):
                seven = rxb.at[t, k, pl.ds(1, 7)]
                remote(seven, seven, ext_sem.at[t, k, 0], ext_sem.at[t, k, 1], second(1)).wait_recv()
                part = dot(unpack_extra(rxb.at[t, k]), wup[k * C : k * C + C])
                total = part if total is None else total + part
            pse[t] = total.astype(BF16)
            extra_products_copy().start()

        for step in range(4):
            for k in range(NC):
                for j in ARRIVALS[step]:
                    ring_copy(k, j).wait_recv()
                    for child in CHILDREN[j]:
                        ring_copy(k, child).start()
            q = step
            for k in range(NC):
                picked = dot(omat[t, q], gb[t, k, 128 * q : 128 * q + 128, :]).astype(BF16).reshape(SIDE, 16, C)
                mb[t, k, q] = picked
                rb[t, k, q, 0] = picked[0]
                for i in FAR_FIRST:
                    main_copy(k, q, i).start()
                if step == 3:
                    pack_extra(dot(o8[t], gb[t, k]), xb.at[t, k])
                    rxb[t, k, 0] = xb[t, k, 0]
                    for i in FAR_FIRST:
                        p = POS[i]
                        remote(xb.at[t, k, p], rxb.at[t, k, p], ext_sem.at[t, k, 0], ext_sem.at[t, k, 1], second(i)).start()
            if step >= 2:
                up_rows(step - 2)
        if t == 0:
            build_maps(0, True)
            for later in range(1, TICKS):
                build_maps(later, False)
                build_maps(later, True)
        up_rows(2)
        up_rows(3)
        up_extra()

        xrow = lax.broadcasted_iota(jnp.int32, (64, 64), 0)
        xlane = lax.broadcasted_iota(jnp.int32, (64, 64), 1)
        swap = jnp.where(xlane == lax.rem(xrow, 8) * 8 + xrow // 8, 1.0, 0.0).astype(BF16)
        for q in range(4):
            products_copy(q).wait_recv()
        extra_products_copy().wait_recv()
        if t == 0:
            down_load.wait()

        def down_extra():
            total = pse[t].astype(F32) + dot(swap, pre[t])
            hidden = silu(total).astype(BF16)
            made = dot(hidden, wdn[...])
            for k in range(NC):
                pack_extra(made[:, k * C : k * C + C], oxb.at[t, k])
                txb[t, k, 0] = oxb[t, k, 0]
                for i in FAR_FIRST:
                    p = POS[i]
                    remote(oxb.at[t, k, p], txb.at[t, k, p], rext_sem.at[t, k, 0], rext_sem.at[t, k, 1], second(-i)).start()

        def down_rows(q):
            parts = []
            for n in range(4):
                block = pr[t, n, 32 * q : 32 * q + 32].astype(F32)
                parts += [block[:8], block[16:24], block[8:16], block[24:]]
            total = ps[t, q].astype(F32) + jnp.concatenate(parts, axis=0)
            hidden = silu(total).astype(BF16)
            for k in range(NC):
                made = dot(hidden, wdn[:, k * C : k * C + C]).astype(BF16).reshape(SIDE, 16, C)
                ob[t, k, q] = made
                tb[t, k, q, 0] = made[0]
                for i in FAR_FIRST:
                    p = POS[i]
                    remote(ob.at[t, k, q, p], tb.at[t, k, q, p], rmain_send.at[t, k], rmain_recv.at[t, k, q], second(-i)).start()

        def back_copy(k, j):
            return remote(
                sb.at[t, k, j], rr.at[t, k, j], back_send.at[t, k], back_recv.at[t, k, j], first(PARENT[j] - j),
            )

        def sum_pair(q):
            squares = jnp.zeros((TOK, 1), F32)
            for k in range(NC):
                if q == 3:
                    seven = txb.at[t, k, pl.ds(1, 7)]
                    remote(seven, seven, rext_sem.at[t, k, 0], rext_sem.at[t, k, 1], second(1)).wait_recv()
                    te[k] = unpack_extra(txb.at[t, k])
                seven = tb.at[t, k, q, pl.ds(1, 7)]
                remote(seven, seven, rmain_send.at[t, k], rmain_recv.at[t, k, q], second(1)).wait_recv()
                part = dot(got[t, q], tb[t, k, q].reshape(128, C))
                part = part + dot(g8t[t, q][:, :64], te[k])
                for h in (1, 0):
                    j = OFFSETS[2 * q + h]
                    total = part[64 * h : 64 * h + 64]
                    for child in CHILDREN[j]:
                        back_copy(k, child).wait_recv()
                        total = total + rr[t, k, child].astype(F32)
                    if j > 0:
                        sb[t, k, j] = total.astype(BF16)
                        back_copy(k, j).start()
                    else:
                        cols = slice(k * C, k * C + C)
                        y = (xn[:, cols].astype(F32) + total).astype(BF16)
                        if t == TICKS - 1:
                            out_ref[:, cols] = y
                        else:
                            shs[t, k] = y

                            @pl.when(pipe < lax.axis_size("pipe") - 1)
                            def _():
                                remote(shs.at[t, k], shr.at[t, k], sh_send.at[t, k], sh_recv.at[t, k], {"pipe": pipe + 1}).start()

                            squares = squares + jnp.sum(y.astype(F32) * y.astype(F32), axis=1, keepdims=True)
                            if k == NC - 1:
                                sqy[t + 1] = jnp.broadcast_to(squares, (TOK, 128))

                                @pl.when(pipe < lax.axis_size("pipe") - 1)
                                def _():
                                    for copy in passed_squares(t + 1, 1):
                                        copy.start()

        down_extra()
        down_rows(3)
        down_rows(2)
        down_rows(1)
        sum_pair(3)
        down_rows(0)
        sum_pair(2)
        sum_pair(1)
        sum_pair(0)

        if t < TICKS - 1:
            if t == 0:
                fresh_load.wait()

            @pl.when(pipe > 0)
            def _():
                for k in range(NC):
                    remote(shs.at[t, k], shr.at[t, k], sh_send.at[t, k], sh_recv.at[t, k], {"pipe": pipe - 1}).wait_recv()
                    xn[:, k * C : k * C + C] = shr[t, k]

            @pl.when(pipe == 0)
            def _():
                xn[...] = fresh_ref[t]
                put_squares(t + 1, fresh_ref[t].astype(F32))
                squares_copy(t + 1).start()
                squares_copy(t + 1).wait()

    seven = pl.ds(1, 7)

    def sent(ref, semaphore):
        pltpu.make_async_remote_copy(
            src_ref=ref, dst_ref=ref, send_sem=semaphore, recv_sem=meta_sem.at[1],
            device_id=other_core, device_id_type=MESH,
        ).wait_send()

    sent(mr.at[seven], meta_sem.at[0])
    for t in range(TICKS):
        for k in range(NC):
            sent(gb.at[t, k, pl.ds(64, 448)], ring_send.at[t, k])
            sent(mb.at[t, k, :, seven], main_send.at[t, k])
            sent(xb.at[t, k, seven], ext_sem.at[t, k, 0])
            sent(ob.at[t, k, :, seven], rmain_send.at[t, k])
            sent(oxb.at[t, k, seven], rext_sem.at[t, k, 0])
            sent(sb.at[t, k, seven], back_send.at[t, k])
        for q in range(4):
            sent(ps.at[t, q], p_sem.at[t, q, 0])
        sent(pse.at[t], pe_sem.at[t, 0])

    @pl.when(pipe < lax.axis_size("pipe") - 1)
    def _():
        for t in range(TICKS - 1):
            for copy in passed_squares(t + 1, 1):
                copy.wait_send()
            for k in range(NC):
                remote(shs.at[t, k], shr.at[t, k], sh_send.at[t, k], sh_recv.at[t, k], {"pipe": pipe + 1}).wait_send()


def on_device(in_flight, fresh_batch, norm_gain, up_weight, down_weight, expert_ids, route_prob):
    ids = jnp.swapaxes(expert_ids[:, 0], 1, 2)
    prob = jnp.swapaxes(route_prob[:, 0], 1, 2)
    hbm = pl.BlockSpec(memory_space=pl.ANY)
    dma = pltpu.SemaphoreType.DMA
    scratch = [
        pltpu.VMEM((TOK, D), BF16),
        pltpu.VMEM(fresh_batch.shape, BF16),
        pltpu.VMEM((1, D), F32),
        pltpu.VMEM((D, HID), BF16),
        pltpu.VMEM((HID, D), BF16),
        pltpu.VMEM((TICKS, TOPK, TOK), jnp.int32),
        pltpu.VMEM((TICKS, TOPK, TOK), F32),
        pltpu.VMEM((TICKS, NC, 512, C), BF16),
        pltpu.VMEM((TICKS, NC, 4, SIDE, 16, C), BF16),
        pltpu.VMEM((TICKS, NC, SIDE, 16, C2), BF16),
        pltpu.VMEM((TICKS, NC, 4, SIDE, 16, C), BF16),
        pltpu.VMEM((TICKS, NC, SIDE, 16, C2), BF16),
        pltpu.VMEM((TICKS, 4, 128, HID), BF16),
        pltpu.VMEM((TICKS, 4, 128, HID), BF16),
        pltpu.VMEM((TICKS, 64, HID), BF16),
        pltpu.VMEM((TICKS, 64, HID), BF16),
        pltpu.VMEM((TICKS, NC, 4, SIDE, 16, C), BF16),
        pltpu.VMEM((TICKS, NC, SIDE, 16, C2), BF16),
        pltpu.VMEM((TICKS, NC, 4, SIDE, 16, C), BF16),
        pltpu.VMEM((TICKS, NC, SIDE, 16, C2), BF16),
        pltpu.VMEM((NC, 64, C), BF16),
        pltpu.VMEM((TICKS, NC, SIDE, TOK, C), BF16),
        pltpu.VMEM((TICKS, NC, SIDE, TOK, C), BF16),
        pltpu.VMEM((TICKS, TOK, 128), F32),
        pltpu.VMEM((TICKS, TOK, 128), F32),
        pltpu.VMEM((TICKS, TOK, 128), F32),
        pltpu.VMEM((TICKS, NC, TOK, C), BF16),
        pltpu.VMEM((TICKS, NC, TOK, C), BF16),
        pltpu.VMEM((SIDE, 32, 128), F32),
        pltpu.VMEM((SIDE, 32, 128), F32),
        pltpu.VMEM((TICKS, 4, 128, 128), BF16),
        pltpu.VMEM((TICKS, 64, 512), BF16),
        pltpu.VMEM((TICKS, 4, 128, 128), BF16),
        pltpu.VMEM((TICKS, 4, 128, 128), BF16),
        dma((7,)), dma((2,)), dma((TICKS, 2)), dma((TICKS, 2)), dma((TICKS, 2)), dma((TICKS, NC)), dma((TICKS, NC)),
        dma((TICKS, NC)), dma((TICKS, NC, SIDE)), dma((TICKS, NC)), dma((TICKS, NC, 4)), dma((TICKS, NC, 2)),
        dma((TICKS, 4, 2)), dma((TICKS, 2)), dma((TICKS, NC)), dma((TICKS, NC, 4)), dma((TICKS, NC, 2)),
        dma((TICKS, NC)), dma((TICKS, NC, SIDE)),
    ]
    y = pl.pallas_call(
        kernel,
        name="window",
        out_shape=jax.ShapeDtypeStruct((TOK, D), BF16),
        in_specs=[hbm] * 7,
        out_specs=pl.BlockSpec(memory_space=pltpu.VMEM),
        scratch_shapes=scratch,
        compiler_params=pltpu.CompilerParams(
            collective_id=0, has_side_effects=True, vmem_limit_bytes=62 * 2**20
        ),
    )(in_flight[0], fresh_batch, norm_gain, up_weight[0, 0], down_weight[0, 0], ids, prob)
    return y[None]


def solution(mesh):
    placed = (
        P("pipe", "expert", "tensor"),
        P(None, "expert", "tensor"),
        P("pipe", "tensor"),
        P("pipe", "expert", "tensor", None),
        P("pipe", "expert", None, "tensor"),
        P(None, "pipe", "expert", None),
        P(None, "pipe", "expert", None),
    )
    return jax.shard_map(
        on_device,
        mesh=mesh,
        in_specs=placed,
        out_specs=P("pipe", "expert", "tensor"),
        check_vma=False,
    )
```
